32 devices in a mesh: groups: 2 (over x), node: 8 (over z, y), outer: 2 (over core).
Axes of the slice: x: 2, y: 2, z: 4, core: 2. Of those that a mesh axis runs over, the one named last changes fastest.
Arguments:
- tokens: bfloat16 [16384, 8192], P(('groups', 'node', 'outer')), parts along dimension 0, may hold values from -6 to 6
- frozen_weight: bfloat16 [8192, 1024], P(('node', 'outer')), may hold values from -0.0625 to 0.0625
- down_adapter: bfloat16 [8192, 128], replicated, may hold values from -0.0625 to 0.0625
- second_adapter_weight: bfloat16 [1024, 128], replicated, may hold values from -0.75 to 0.75
- tenant_ids: int32 [128], P(('groups', 'node', 'outer')), parts along dimension 0, may hold values from 0 to 7
- block_counts: int32 [32], P(('groups', 'node', 'outer')), parts along dimension 0, may hold values from 1 to 4, as said below
- positions: int32 [16384], P(('groups', 'node', 'outer')), parts along dimension 0, may hold values from 0 to 4095, as said below
- cotangent: bfloat16 [16384, 1024], P(('groups', 'node', 'outer')), parts along dimension 0, may hold values from -6 to 6
Outputs:
- keys: bfloat16 [16384, 1024], P(('groups', 'node', 'outer')), parts along dimension 0
- down_adapter_gradient: float32 [16384, 128], P(('groups', 'node')), parts along dimension 0
- up_adapter_gradient: float32 [2048, 128], P(('groups', 'node')), parts along dimension 0
The draws below stay inside these ranges and needn't reach their ends.
There are 2 independent parts, one for each index of `groups`. The reference program is written for one: setup_inputs(seed, part) draws one part's arguments, and reference() takes and returns one part's arrays. A program takes and returns all parts, laid end to end along the dimension named above; an argument that names none is the same for every part. Nothing has to cross between parts.
Inputs may be any that keep to these rules, and one draw needn't show every extreme that they name: `block_counts`: each device's live blocks come first among its 4 blocks; some device has all live. Each block of 128 tokens holds consecutive positions starting at a multiple of 128.
All inputs are finite; a program needn't handle non-finite values.
Results may differ from the reference program's by a relative error of at most 0.0051.
Values may be sent and summed in bfloat16 or wider, within the bound.
No kernel may reach another device: no remote copies, remote signals or barrier semaphores. Data moves between devices by JAX's collectives and lax.ppermute only.
A program may use at most 128 MiB of HBM per device.

```python
import jax
import jax.numpy as jnp

D = 8192
HEAD = 128
R = 16
TEN = 8
BLK = 128
SEQ = 4096
BLK_DEV = 4
KV = 1024
GROUP = 16
BLOCKS = 64
TOKENS = 8192


def draw_block_counts(key, part):
    key = jax.random.fold_in(key, 11)
    first_key, second_key = jax.random.split(key)
    counted = jax.random.randint(first_key, (GROUP,), 1, BLK_DEV + 1)
    chosen = jax.random.randint(second_key, (), 0, GROUP)
    return jnp.where(jnp.arange(GROUP) == chosen, BLK_DEV, counted).astype(jnp.int32)


def draw_positions(key, part):
    key = jax.random.fold_in(key, 23)
    first_key, second_key = jax.random.split(key)
    starts = jax.random.randint(first_key, (BLOCKS,), 0, SEQ // BLK) * BLK
    chosen = jax.random.randint(second_key, (), 0, BLOCKS)
    starts = jnp.where(jnp.arange(BLOCKS) == chosen, SEQ - BLK, starts)
    return (starts[:, None] + jnp.arange(BLK)[None, :]).reshape(TOKENS).astype(jnp.int32)


def place_ends(values, rng, least, largest):
    dims = values.shape
    spot = [jax.random.randint(jax.random.fold_in(rng, axis), (), 0, dims[axis]) for axis in range(len(dims))]
    values = values.at[tuple(spot)].set(least)
    longest = dims.index(max(dims))
    spot[longest] = (spot[longest] + 1) % dims[longest]
    return values.at[tuple(spot)].set(largest)


def block_scale(rng, extent, pieces, low, top_value):
    level = 1.0
    for position, parts in pieces:
        steps = jax.random.uniform(jax.random.fold_in(jax.random.fold_in(rng, 6), position), (parts,), jnp.float32, low / len(pieces), top_value / len(pieces))
        level = level * jnp.repeat(jnp.exp(steps), extent[position] // parts).reshape((-1,) + (1,) * (len(extent) - 1 - position))
    return level


def noise(own_key, extent, scale, bound, cuts=(), held_as=jnp.bfloat16):
    gain = block_scale(own_key, extent, cuts, -0.22, 0.18) if cuts else 1.0
    result = jax.random.normal(own_key, extent, jnp.float32) * scale * gain
    return jnp.minimum(jnp.maximum(result, -bound), bound).astype(held_as)


def setup_inputs(seed: int = 0, part: int = 0) -> dict:
    splits = jax.random.split(jax.random.key(seed), 9)
    own_keys = jax.random.split(jax.random.fold_in(splits[8], part), 9)
    tokens = noise(own_keys[0], (TOKENS, D), 1.0, 6.0, ((0, 16),))
    frozen_weight = noise(splits[1], (D, KV), D ** -0.5, 0.0625, ((0, 16),))
    down_adapter = noise(splits[2], (D, TEN * R), D ** -0.5, 0.0625)
    second_adapter_weight = noise(splits[3], (KV, TEN * R), (4 * R) ** -0.5, 0.75)
    tenant_ids = place_ends(jax.random.randint(own_keys[4], (BLOCKS,), 0, TEN), jax.random.fold_in(own_keys[4], 1), 0, TEN - 1).astype(jnp.int32)
    block_counts = draw_block_counts(jax.random.fold_in(jax.random.fold_in(splits[8], part), 71), part)
    positions = draw_positions(jax.random.fold_in(jax.random.fold_in(splits[8], part), 71), part)
    cotangent = noise(own_keys[7], (TOKENS, KV), 1.0, 6.0, ((0, 16),))
    return {"tokens": tokens, "frozen_weight": frozen_weight, "down_adapter": down_adapter, "second_adapter_weight": second_adapter_weight, "tenant_ids": tenant_ids, "block_counts": block_counts, "positions": positions, "cotangent": cotangent}


ROPE_BASE = 500000.0
ADAPTER_SCALE = 2.0


def rope_tables(positions):
    half_head = HEAD // 2
    frequency = ROPE_BASE ** (-2.0 * jnp.arange(half_head, dtype=jnp.float32) / HEAD)
    angle = positions.astype(jnp.float32)[:, None] * frequency[None, :]
    return jnp.cos(angle), jnp.sin(angle)


def rotate(field, cosine, sine, orient):
    rows = field.shape[0]
    shaped = field.reshape(rows, -1, 2, HEAD // 2)
    first = shaped[:, :, 0]
    second = shaped[:, :, 1]
    cos_b = cosine[:, None, :]
    sin_b = orient * sine[:, None, :]
    out_first = first * cos_b - second * sin_b
    out_second = second * cos_b + first * sin_b
    return jnp.stack((out_first, out_second), axis=2).reshape(rows, -1)


def reference(tokens, frozen_weight, down_adapter, second_adapter_weight, tenant_ids, block_counts, positions, cotangent):
    block_index = jnp.arange(BLOCKS, dtype=jnp.int32)
    owner = block_index // BLK_DEV
    local_index = block_index % BLK_DEV
    live_blocks = (local_index < block_counts[owner]).astype(jnp.float32)
    live_rows = jnp.repeat(live_blocks, BLK)[:, None]
    column_tenant = jnp.arange(TEN * R, dtype=jnp.int32) // R
    select_blocks = (tenant_ids[:, None] == column_tenant[None, :]).astype(jnp.float32) * live_blocks[:, None]
    select = jnp.repeat(select_blocks, BLK, axis=0)
    lowrank_hidden = (jnp.dot(tokens, down_adapter, preferred_element_type=jnp.float32) * select).astype(jnp.bfloat16)
    unrotated_keys = jnp.dot(tokens, frozen_weight, preferred_element_type=jnp.float32)
    unrotated_keys = unrotated_keys + ADAPTER_SCALE * jnp.dot(lowrank_hidden, second_adapter_weight.T, preferred_element_type=jnp.float32)
    cosine, sine = rope_tables(positions)
    keys = (live_rows * rotate(unrotated_keys, cosine, sine, 1.0)).astype(jnp.bfloat16)
    output_gradient = (live_rows * rotate(cotangent.astype(jnp.float32), cosine, sine, -1.0)).astype(jnp.bfloat16)
    backward_gradient = (jnp.dot(output_gradient, second_adapter_weight, preferred_element_type=jnp.float32) * select).astype(jnp.bfloat16)
    down_adapter_gradient = ADAPTER_SCALE * jnp.dot(tokens.T, backward_gradient, preferred_element_type=jnp.float32)
    up_adapter_gradient = ADAPTER_SCALE * jnp.dot(output_gradient.T, lowrank_hidden, preferred_element_type=jnp.float32)
    return keys, down_adapter_gradient, up_adapter_gradient
```

```python
import functools

import jax
import jax.numpy as jnp
import numpy as np
from jax import lax
from jax.experimental import pallas as pl
from jax.experimental.pallas import tpu as pltpu
from jax.sharding import PartitionSpec as P

HEAD = 128
R = 16
BLK = 128
SEQ = 4096
ROPE_BASE = 500000.0
ADAPTER_SCALE = 2.0
ALL = ("groups", "node", "outer")
ANY = pl.BlockSpec(memory_space=pl.ANY)
VMEM_LIMIT = 48 * 1024 * 1024


def rope_constants():
    half = HEAD // 2
    frequency = ROPE_BASE ** (-2.0 * np.arange(half) / HEAD)
    inside = np.arange(BLK)[:, None] * frequency[None, :]
    starts = BLK * np.arange(SEQ // BLK)[:, None] * frequency[None, :]
    both = lambda t: np.concatenate((t, t), axis=1)
    return np.concatenate(
        (both(np.cos(inside)), both(np.sin(inside)), both(np.cos(starts)), both(np.sin(starts)))
    ).astype(np.float32)


def block_tables(tab_ref, c_row, s_row):
    c_in = tab_ref[0:BLK, :]
    s_in = tab_ref[BLK : 2 * BLK, :]
    cosine = c_in * c_row - s_in * s_row
    sine = s_in * c_row + c_in * s_row
    lane = lax.broadcasted_iota(jnp.int32, (1, HEAD), 1)
    return cosine, jnp.where(lane < HEAD // 2, -sine, sine)


def gradient_kernel(
    sc, tids, count, pos, tok_ref, a_ref, b_ref, cot_ref, tab_ref,
    low_ref, own_ref, sib_ref, grad, back, acc, piece,
):
    step = pl.program_id(0)
    slots = pl.num_programs(0)
    chunk = tok_ref.shape[1]
    kv = cot_ref.shape[1]
    blocks = tok_ref.shape[0] // BLK
    up_rows = kv // slots
    down_half, up_half = chunk // 2, up_rows // 2
    outer = sc[8]
    lane = lax.broadcasted_iota(jnp.int32, (1, HEAD), 1)

    def select(b):
        hit = jnp.logical_and(lane // R == tids[b], b < count[0])
        return jnp.where(hit, 1.0, 0.0).astype(jnp.float32)

    @pl.when(step == 0)
    def _():
        acc[...] = jnp.zeros_like(acc)
        for b in range(blocks):
            rows = slice(b * BLK, (b + 1) * BLK)
            start = pos[b * BLK] // BLK
            cosine, sine = block_tables(
                tab_ref,
                tab_ref[pl.ds(2 * BLK + start, 1), :],
                tab_ref[pl.ds(2 * BLK + SEQ // BLK + start, 1), :],
            )
            live = jnp.where(b < count[0], 1.0, 0.0).astype(jnp.float32)
            for h in range(kv // HEAD):
                cols = slice(h * HEAD, (h + 1) * HEAD)
                x = cot_ref[rows, cols].astype(jnp.float32)
                g = x * cosine - pltpu.roll(x, HEAD // 2, 1) * sine
                grad[rows, cols] = (live * g).astype(jnp.bfloat16)
            back[rows, :] = (
                jnp.dot(grad[rows, :], b_ref[...], preferred_element_type=jnp.float32) * select(b)
            ).astype(jnp.bfloat16)

    tok = tok_ref[...]
    acc[...] += jnp.dot(tok, a_ref[...], preferred_element_type=jnp.float32)
    piece[...] = ADAPTER_SCALE * lax.dot_general(
        tok, back[...], (((0,), (0,)), ((), ())), preferred_element_type=jnp.float32
    )
    own_ref[step, 0:down_half, :] = piece[pl.ds(outer * down_half, down_half), :]
    sib_ref[step, 0:down_half, :] = piece[
        pl.ds((1 - outer) * down_half, down_half), :
    ].astype(jnp.bfloat16)

    @pl.when(step == slots - 1)
    def _():
        for b in range(blocks):
            rows = slice(b * BLK, (b + 1) * BLK)
            low_ref[rows, :] = (acc[rows, :] * select(b)).astype(jnp.bfloat16)
        note = jnp.zeros((1, HEAD), jnp.int32)
        for b in range(blocks):
            note = jnp.where(lane == b, pos[b * BLK] // BLK, note)
        note = jnp.where(lane == blocks, count[0], note)
        low_ref[blocks * BLK :, :] = jnp.broadcast_to(
            note.astype(jnp.float32), (16, HEAD)
        ).astype(jnp.bfloat16)
        piece[0:kv, :] = ADAPTER_SCALE * lax.dot_general(
            grad[...], low_ref[0 : blocks * BLK, :], (((0,), (0,)), ((), ())),
            preferred_element_type=jnp.float32,
        )
        for r in range(slots):
            base = sc[r] * up_rows
            own_ref[r, down_half:, :] = piece[pl.ds(base + outer * up_half, up_half), :]
            sib_ref[r, down_half:, :] = piece[
                pl.ds(base + (1 - outer) * up_half, up_half), :
            ].astype(jnp.bfloat16)


def first_kernel(spec, common, sc, w_ref, r_ref, out_ref, sems):
    rows, half = r_ref.shape
    plane, outer = sc[9], sc[8]
    tail = spec + common - rows

    def gather(p, o):
        mine = w_ref.at[:, o * half : (o + 1) * half]
        lower, upper = (mine, r_ref) if o == 0 else (r_ref, mine)
        if p == 0:
            moves = ((lower, 0, rows, 0), (upper, 0, tail, rows))
        else:
            moves = (
                (upper, rows - spec, spec, 0),
                (lower, spec, rows - spec, spec),
                (upper, 0, tail, rows),
            )
        copies = [
            pltpu.make_async_copy(
                src.at[at : at + n, :], out_ref.at[to : to + n, :], sems.at[i]
            )
            for i, (src, at, n, to) in enumerate(moves)
        ]
        for c in copies:
            c.start()
        for c in copies:
            c.wait()

    for p in range(2):
        for o in range(2):
            pl.when(jnp.logical_and(plane == p, outer == o))(functools.partial(gather, p, o))


def sources_of(kind, sc, chunk, spec, common, refs):
    plane, outer = sc[9], sc[8]
    mine, theirs = plane * (spec + common), (1 - plane) * (spec + common)
    node = lambda i: sc[i] * chunk

    def whole(i, held, crossed, at):
        return (
            node(i), chunk,
            ((held, 0, spec, mine), (held, spec, common, spec), (crossed, at, spec, theirs)),
        )

    if kind == 0:
        w_ref, r_ref, y0, x1, z1 = refs
        rows = r_ref.shape[0]
        half = r_ref.shape[1]
        own = w_ref.at[:, pl.ds(pl.multiple_of(outer * half, half), half)]
        return (
            (node(10), chunk, ((own, 0, rows, outer * rows), (r_ref, 0, rows, (1 - outer) * rows))),
            whole(14, y0, x1, 0),
            whole(11, z1, x1, spec),
        )
    if kind == 1:
        y1, x2, z2 = refs
        return (whole(15, y1, x2, 0), whole(12, z2, x2, spec))
    if kind == 2:
        y2, x3, z3, y3 = refs
        return (
            whole(16, y2, x3, 0),
            whole(13, z3, x3, spec),
            (
                node(17) + plane * spec, spec + common,
                ((y3, 0, spec, plane * common), (y3, spec, common, (1 - plane) * spec)),
            ),
        )
    (x4,) = refs
    return ((node(17) + theirs, spec, ((x4, 0, spec, 0),)),)


def load_sources(sources, toks, tv, wv, sems):
    at, copies = 0, []
    for first, width, pieces in sources:
        first = pl.multiple_of(first, 128)
        for i, t in enumerate(toks):
            copies.append((t.at[:, pl.ds(first, width)], tv.at[i, :, at : at + width]))
        for ref, row, n, to in pieces:
            to = pl.multiple_of(at + to, 128)
            copies.append((ref.at[row : row + n, :], wv.at[pl.ds(to, n), :]))
        at += width
    made = [pltpu.make_async_copy(s, d, sems.at[i]) for i, (s, d) in enumerate(copies)]
    for c in made:
        c.start()
    return made


def product_kernel(kind, spec, common, sc, *refs):
    refs, (out_ref, tv, wv, sems, step_sems) = refs[:-5], refs[-5:]
    toks, extra, pieces = refs[:2], refs[2:5] if kind == 0 else refs[2:3], refs[5:] if kind == 0 else refs[3:]
    chunk = toks[0].shape[1] // 8
    sources = sources_of(kind, sc, chunk, spec, common, pieces)
    made = load_sources(sources, toks, tv, wv, sems)
    if kind:
        total = pltpu.make_async_copy(extra[0], out_ref, step_sems.at[0])
        total.start()
        total.wait()
    for c in made:
        c.wait()
    tokens = out_ref.shape[1]
    half = out_ref.shape[2]
    block = 256

    @pl.loop(0, 2 * (tokens // block))
    def _(i):
        core = i // (tokens // block)
        rows = pl.ds(pl.multiple_of(lax.rem(i, tokens // block) * block, block), block)
        if kind:
            start = out_ref[core, rows, :]
        else:
            low, low_s, b_ref = extra
            lows = jnp.where(core == 0, low[rows, :], low_s[rows, :])
            start = ADAPTER_SCALE * lax.dot_general(
                lows, b_ref[pl.ds(pl.multiple_of(sc[8] * half, half), half), :],
                (((1,), (1,)), ((), ())), preferred_element_type=jnp.float32,
            )
        out_ref[core, rows, :] = start + jnp.dot(
            tv[core, rows, :], wv[...], preferred_element_type=jnp.float32
        )


def finish_kernel(core, spec, common, sc, tok, total_ref, low_ref, tab_ref, x4, out_ref, tv, wv, tot, res, sems):
    chunk = tok.shape[1] // 8
    sources = sources_of(3, sc, chunk, spec, common, (x4,))
    made = load_sources(sources, (tok,), tv, wv, sems)
    total = pltpu.make_async_copy(total_ref.at[core], tot, sems.at[3])
    total.start()
    tokens, half = tot.shape
    note = low_ref[tokens:, :].astype(jnp.float32)[0:1, :]
    starts = SEQ // BLK
    index = lax.broadcasted_iota(jnp.int32, (starts, HEAD), 0).astype(jnp.float32)
    blocks = tokens // BLK
    tables = []
    for b in range(blocks):
        hit = index == note[:, b : b + 1]
        pick = lambda at: jnp.sum(
            jnp.where(hit, tab_ref[at : at + starts, :], 0.0), axis=0, keepdims=True
        )
        tables.append(block_tables(tab_ref, pick(2 * BLK), pick(2 * BLK + starts)))
    for c in made:
        c.wait()
    total.wait()
    for b in range(blocks):
        rows = slice(b * BLK, (b + 1) * BLK)
        cosine, sine = tables[b]
        live = jnp.where(note[:, blocks : blocks + 1] > b, 1.0, 0.0)
        cosine, sine = cosine * live, sine * live
        pre = tot[rows, :] + jnp.dot(tv[0, rows, :], wv[...], preferred_element_type=jnp.float32)
        for h in range(half // HEAD):
            cols = slice(h * HEAD, (h + 1) * HEAD)
            x = pre[:, cols]
            res[rows, cols] = (x * cosine + pltpu.roll(x, HEAD // 2, 1) * sine).astype(jnp.bfloat16)
    if core:
        dst = out_ref
    else:
        dst = out_ref.at[:, pl.ds(pl.multiple_of(sc[8] * half, half), half)]
    save = pltpu.make_async_copy(res, dst, sems.at[3])
    save.start()
    save.wait()


def merge_kernel(sc, given_ref, keys_ref, out_ref, sem):
    half = given_ref.shape[1]
    at = pl.multiple_of((1 - sc[8]) * half, half)
    move = pltpu.make_async_copy(given_ref, out_ref.at[:, pl.ds(at, half)], sem)
    move.start()
    move.wait()


class Routes:
    def __init__(self, mesh):
        self.groups, self.nodes, self.outers = (mesh.shape[a] for a in ALL)
        self.z = self.nodes // 2
        line = list(range(self.z))
        ring = line[:1] + line[1::2] + line[2::2][::-1]
        self.next = {ring[i]: ring[(i + 1) % self.z] for i in range(self.z)}
        self.prev = {v: k for k, v in self.next.items()}

    def pairs(self, f):
        at = lambda g, z, y, o: (g * self.nodes + 2 * z + y) * self.outers + o
        return [
            (at(g, z, y, o), at(*f(g, z, y, o)))
            for g in range(self.groups)
            for z in range(self.z)
            for y in range(2)
            for o in range(self.outers)
        ]

    def table(self):
        rows = []
        for _, n, o, g in [
            (0, n, o, g) for g in range(self.groups) for n in range(self.nodes) for o in range(self.outers)
        ]:
            z, y = divmod(n, 2)
            slot = [n ^ (((r >> 2) & 1) | (((r >> 1) & 1) << 1) | ((r & 1) << 2)) for r in range(8)]
            from_z = [z]
            for _ in range(self.z - 1):
                from_z.append(self.prev[from_z[-1]])
            rows.append(
                slot + [o, g] + [2 * k + y for k in from_z] + [2 * k + 1 - y for k in from_z]
            )
        return np.array(rows, np.int32)


def call(kernel, name, shapes, in_specs, out_specs, scratch, args, grid=(), prefetch=1, flops=0, moved=0, aliases=None):
    return pl.pallas_call(
        kernel,
        out_shape=shapes,
        grid_spec=pltpu.PrefetchScalarGridSpec(
            num_scalar_prefetch=prefetch, grid=grid, in_specs=in_specs, out_specs=out_specs,
            scratch_shapes=scratch,
        ),
        compiler_params=pltpu.CompilerParams(vmem_limit_bytes=VMEM_LIMIT),
        cost_estimate=pl.CostEstimate(flops=flops, bytes_accessed=moved, transcendentals=0),
        input_output_aliases=aliases or {},
        name=name,
    )(*args)


def fast_body(
    routes, tokens, frozen_weight, down_adapter, second_adapter_weight, tenant_ids, block_counts, positions, cotangent
):
    bf16, f32 = jnp.bfloat16, jnp.float32
    rows, width = tokens.shape
    weight_rows, kv = frozen_weight.shape
    half = kv // 2
    nodes = routes.nodes
    chunk = 2 * weight_rows
    spec, common = 3 * chunk // 8, chunk // 4
    held = spec + common
    rank = down_adapter.shape[1]
    outer = lax.axis_index("outer")
    me = lax.axis_index(ALL)
    table = routes.table()
    sc = lax.dynamic_slice(jnp.asarray(table), (me, 0), (1, table.shape[1]))[0]
    tab = jnp.asarray(rope_constants())

    send = lambda x, f: lax.ppermute(x, ALL, routes.pairs(f))
    to_core = lambda g, z, y, o: (g, z, y, 1 - o)
    to_x = lambda g, z, y, o: (1 - g, z, y, o)
    to_y = lambda g, z, y, o: (g, z, 1 - y, o)
    to_z = lambda g, z, y, o: (g, routes.next[z], y, o)
    to_z1 = lambda g, z, y, o: (g, z ^ 1, y, o)
    to_z2 = lambda g, z, y, o: (g, z ^ 2, y, o)
    vm = pl.BlockSpec(memory_space=pltpu.VMEM)
    dma = pltpu.SemaphoreType.DMA
    shape = jax.ShapeDtypeStruct

    other = lax.dynamic_slice(frozen_weight, (0, (1 - outer) * half), (weight_rows, half))
    r = send(other, to_core)
    z0 = call(
        functools.partial(first_kernel, spec, common), "first_rows", shape((held, half), bf16),
        [ANY, ANY], vm, [dma((3,))], (sc, frozen_weight, r), moved=4 * held * half,
    )
    z1 = send(z0, to_z)
    y0 = send(z0, to_y)
    sib_tokens = send(tokens, to_core)

    slot_rows = chunk // 2 + kv // nodes // 2
    low, own, sib = call(
        gradient_kernel, "adapter_gradients",
        (
            shape((rows + 16, rank), bf16),
            shape((nodes, slot_rows, rank), f32),
            shape((nodes, slot_rows, rank), bf16),
        ),
        [
            pl.BlockSpec((rows, chunk), lambda i, sc, *_: (0, sc[i])),
            pl.BlockSpec((chunk, rank), lambda i, sc, *_: (sc[i], 0)),
            pl.BlockSpec((kv, rank), lambda i, *_: (0, 0)),
            pl.BlockSpec((rows, kv), lambda i, *_: (0, 0)),
            pl.BlockSpec(tab.shape, lambda i, *_: (0, 0)),
        ],
        (
            pl.BlockSpec((rows + 16, rank), lambda i, *_: (0, 0)),
            pl.BlockSpec((nodes, slot_rows, rank), lambda i, *_: (0, 0, 0)),
            pl.BlockSpec((nodes, slot_rows, rank), lambda i, *_: (0, 0, 0)),
        ),
        [
            pltpu.VMEM((rows, kv), bf16),
            pltpu.VMEM((rows, rank), bf16),
            pltpu.VMEM((rows, rank), f32),
            pltpu.VMEM((max(chunk, kv), rank), f32),
        ],
        (sc, tenant_ids, block_counts, positions, tokens, down_adapter, second_adapter_weight, cotangent, tab),
        grid=(nodes,), prefetch=4,
        flops=2 * rows * rank * (2 * width + 2 * kv), moved=2 * rows * width + 2 * width * rank + 6 * nodes * slot_rows * rank,
    )
    low_s = send(low, to_core)
    s = own + send(sib, to_core).astype(f32)
    s = s[:4] + send(s[4:].astype(bf16), to_y).astype(f32)

    crossed = lambda y, z: send(jnp.concatenate((y[:spec], z[:spec])), to_x)
    z2 = send(z1, to_z)
    y1 = send(z1, to_y)
    x1 = crossed(y0, z1)
    z3 = send(z2, to_z)
    y2 = send(z2, to_y)
    x2 = crossed(y1, z2)
    y3 = send(z3, to_y)
    x3 = crossed(y2, z3)
    x4 = send(y3[:spec], to_x)

    s = s[:2] + send(s[2:].astype(bf16), to_z1).astype(f32)
    s = s[0] + send(s[1].astype(bf16), to_z2).astype(f32)
    t = send(s, to_core)

    def product(kind, depth, copies, extra, extra_specs, pieces):
        return call(
            functools.partial(product_kernel, kind, spec, common), "product_%d" % kind,
            shape((2, rows, half), f32),
            [ANY, ANY, *extra_specs, *[ANY] * len(pieces)], vm,
            [pltpu.VMEM((2, rows, depth), bf16), pltpu.VMEM((depth, half), bf16), dma((copies,)), dma((1,))],
            (sc, tokens, sib_tokens, *extra, *pieces),
            flops=4 * rows * depth * half, moved=4 * rows * depth + 2 * depth * half + 16 * rows * half,
        )

    total = product(
        0, 3 * chunk, 14, (low, low_s, second_adapter_weight), (vm, vm, vm), (frozen_weight, r, y0, x1, z1)
    )
    total = product(1, 2 * chunk, 10, (total,), (ANY,), (y1, x2, z2))
    total = product(2, 2 * chunk + held, 14, (total,), (ANY,), (y2, x3, z3, y3))

    def finish(core, out, tok, lows):
        return call(
            functools.partial(finish_kernel, core, spec, common), "finish_%d" % core, out,
            [ANY, ANY, vm, vm, ANY], ANY,
            [
                pltpu.VMEM((1, rows, spec), bf16), pltpu.VMEM((spec, half), bf16),
                pltpu.VMEM((rows, half), f32), pltpu.VMEM((rows, half), bf16), dma((4,)),
            ],
            (sc, tok, total, lows, tab, x4),
            flops=2 * rows * spec * half, moved=6 * rows * half + 2 * rows * spec,
        )

    theirs = finish(1, shape((rows, half), bf16), sib_tokens, low_s)
    given = send(theirs, to_core)
    mine = finish(0, shape((rows, kv), bf16), tokens, low)
    keys = call(
        merge_kernel, "merge", shape((rows, kv), bf16), [ANY, ANY], ANY, [dma],
        (sc, given, mine), aliases={2: 0}, moved=4 * rows * half,
    )
    down_rows = chunk // 2
    lower, upper = jnp.where(outer == 0, s, t), jnp.where(outer == 0, t, s)
    down = jnp.concatenate((lower[:down_rows], upper[:down_rows]))
    up = jnp.concatenate((lower[down_rows:], upper[down_rows:]))
    return keys, down, up


def rope_tables(positions):
    half_head = HEAD // 2
    frequency = ROPE_BASE ** (-2.0 * jnp.arange(half_head, dtype=jnp.float32) / HEAD)
    angle = positions.astype(jnp.float32)[:, None] * frequency[None, :]
    return (jnp.cos(angle), jnp.sin(angle))


def rotate(field, cosine, sine, orient):
    rows = field.shape[0]
    shaped = field.reshape(rows, -1, 2, HEAD // 2)
    first = shaped[:, :, 0]
    second = shaped[:, :, 1]
    cos_b = cosine[:, None, :]
    sin_b = orient * sine[:, None, :]
    out_first = first * cos_b - second * sin_b
    out_second = second * cos_b + first * sin_b
    return jnp.stack((out_first, out_second), axis=2).reshape(rows, -1)


def plain_body(
    tokens, frozen_weight, down_adapter, second_adapter_weight, tenant_ids, block_counts, positions, cotangent
):
    token_rows = tokens.shape[0]
    block_total = tenant_ids.shape[0]
    block_rows = token_rows // block_total
    width_cols = down_adapter.shape[1]
    live_blocks = (jnp.arange(block_total, dtype=jnp.int32) < block_counts[0]).astype(jnp.float32)
    live_rows = jnp.repeat(live_blocks, block_rows)[:, None]
    column_tenant = jnp.arange(width_cols, dtype=jnp.int32) // R
    select_blocks = (tenant_ids[:, None] == column_tenant[None, :]).astype(
        jnp.float32
    ) * live_blocks[:, None]
    select = jnp.repeat(select_blocks, block_rows, axis=0)
    lowrank_hidden = (
        jnp.dot(tokens, down_adapter, preferred_element_type=jnp.float32) * select
    ).astype(jnp.bfloat16)
    frozen_output = jnp.dot(
        tokens,
        lax.all_gather(frozen_weight, ("node", "outer"), axis=0, tiled=True),
        preferred_element_type=jnp.float32,
    )
    adapter_output = lax.dot_general(
        lowrank_hidden,
        second_adapter_weight,
        (((1,), (1,)), ((), ())),
        preferred_element_type=jnp.float32,
    )
    unrotated_keys = frozen_output + ADAPTER_SCALE * adapter_output
    cosine, sine = rope_tables(positions)
    keys = (live_rows * rotate(unrotated_keys, cosine, sine, 1.0)).astype(jnp.bfloat16)
    output_gradient = (
        live_rows * rotate(cotangent.astype(jnp.float32), cosine, sine, -1.0)
    ).astype(jnp.bfloat16)
    backward_gradient = (
        jnp.dot(output_gradient, second_adapter_weight, preferred_element_type=jnp.float32) * select
    ).astype(jnp.bfloat16)
    down_product = ADAPTER_SCALE * lax.dot_general(
        tokens, backward_gradient, (((0,), (0,)), ((), ())), preferred_element_type=jnp.float32
    )
    up_product = ADAPTER_SCALE * lax.dot_general(
        output_gradient,
        lowrank_hidden,
        (((0,), (0,)), ((), ())),
        preferred_element_type=jnp.float32,
    )
    shares = (
        lax.psum_scatter(down_product, "node", scatter_dimension=0, tiled=True),
        lax.psum_scatter(up_product, "node", scatter_dimension=0, tiled=True),
    )
    down_adapter_gradient, up_adapter_gradient = lax.psum((shares[0], shares[1]), "outer")
    return (keys, down_adapter_gradient, up_adapter_gradient)


def solution(mesh):
    placed = (
        P(("groups", "node", "outer"), None),
        P(("node", "outer"), None),
        P(),
        P(),
        P(("groups", "node", "outer")),
        P(("groups", "node", "outer")),
        P(("groups", "node", "outer")),
        P(("groups", "node", "outer"), None),
    )
    routed = tuple(mesh.shape[a] for a in ALL) == (2, 8, 2)
    return jax.shard_map(
        functools.partial(fast_body, Routes(mesh)) if routed else plain_body,
        mesh=mesh,
        in_specs=placed,
        out_specs=(
            P(("groups", "node", "outer"), None),
            P(("groups", "node"), None),
            P(("groups", "node"), None),
        ),
        check_vma=False,
    )
```

```python
import functools

import jax
import jax.numpy as jnp
import numpy as np
from jax import lax
from jax.experimental import pallas as pl
from jax.experimental.pallas import tpu as pltpu
from jax.sharding import PartitionSpec as P

HEAD = 128
R = 16
BLK = 128
SEQ = 4096
ROPE_BASE = 500000.0
ADAPTER_SCALE = 2.0
ALL = ("groups", "node", "outer")
ANY = pl.BlockSpec(memory_space=pltpu.HBM)
VMEM_LIMIT = 56 * 1024 * 1024


def rope_constants():
    half = HEAD // 2
    frequency = ROPE_BASE ** (-2.0 * np.arange(half) / HEAD)
    inside = np.arange(BLK)[:, None] * frequency[None, :]
    starts = BLK * np.arange(SEQ // BLK)[:, None] * frequency[None, :]
    both = lambda t: np.concatenate((t, t), axis=1)
    return np.concatenate(
        (both(np.cos(inside)), both(np.sin(inside)), both(np.cos(starts)), both(np.sin(starts)))
    ).astype(np.float32)


def block_tables(tab_ref, c_row, s_row):
    c_in = tab_ref[0:BLK, :]
    s_in = tab_ref[BLK : 2 * BLK, :]
    cosine = c_in * c_row - s_in * s_row
    sine = s_in * c_row + c_in * s_row
    lane = lax.broadcasted_iota(jnp.int32, (1, HEAD), 1)
    return cosine, jnp.where(lane < HEAD // 2, -sine, sine)


def gradient_kernel(
    sc, tids, count, pos, tok_ref, a_ref, b_ref, cot_ref, tab_ref,
    low_ref, own_ref, sib_ref, grad, back, acc, piece,
):
    step = pl.program_id(0)
    slots = pl.num_programs(0)
    chunk = tok_ref.shape[1]
    kv = cot_ref.shape[1]
    blocks = tok_ref.shape[0] // BLK
    up_rows = kv // slots
    down_half, up_half = chunk // 2, up_rows // 2
    outer = sc[8]
    lane = lax.broadcasted_iota(jnp.int32, (1, HEAD), 1)

    def select(b):
        hit = jnp.logical_and(lane // R == tids[b], b < count[0])
        return jnp.where(hit, 1.0, 0.0).astype(jnp.float32)

    @pl.when(step == 0)
    def _():
        acc[...] = jnp.zeros_like(acc)
        for b in range(blocks):
            rows = slice(b * BLK, (b + 1) * BLK)
            start = pos[b * BLK] // BLK
            cosine, sine = block_tables(
                tab_ref,
                tab_ref[pl.ds(2 * BLK + start, 1), :],
                tab_ref[pl.ds(2 * BLK + SEQ // BLK + start, 1), :],
            )
            live = jnp.where(b < count[0], 1.0, 0.0).astype(jnp.float32)
            for h in range(kv // HEAD):
                cols = slice(h * HEAD, (h + 1) * HEAD)
                x = cot_ref[rows, cols].astype(jnp.float32)
                g = x * cosine - pltpu.roll(x, HEAD // 2, 1) * sine
                grad[rows, cols] = (live * g).astype(jnp.bfloat16)
            back[rows, :] = (
                jnp.dot(grad[rows, :], b_ref[...], preferred_element_type=jnp.float32) * select(b)
            ).astype(jnp.bfloat16)

    tok = tok_ref[...]
    acc[...] += jnp.dot(tok, a_ref[...], preferred_element_type=jnp.float32)
    piece[...] = ADAPTER_SCALE * lax.dot_general(
        tok, back[...], (((0,), (0,)), ((), ())), preferred_element_type=jnp.float32
    )
    own_ref[step, 0:down_half, :] = piece[pl.ds(outer * down_half, down_half), :]
    sib_ref[step, 0:down_half, :] = piece[
        pl.ds((1 - outer) * down_half, down_half), :
    ].astype(jnp.bfloat16)

    @pl.when(step == slots - 1)
    def _():
        for b in range(blocks):
            rows = slice(b * BLK, (b + 1) * BLK)
            low_ref[rows, :] = (acc[rows, :] * select(b)).astype(jnp.bfloat16)
        piece[0:kv, :] = ADAPTER_SCALE * lax.dot_general(
            grad[...], low_ref[...], (((0,), (0,)), ((), ())),
            preferred_element_type=jnp.float32,
        )
        for r in range(slots):
            base = sc[r] * up_rows
            own_ref[r, down_half:, :] = piece[pl.ds(base + outer * up_half, up_half), :]
            sib_ref[r, down_half:, :] = piece[
                pl.ds(base + (1 - outer) * up_half, up_half), :
            ].astype(jnp.bfloat16)


def product_kernel(held_from, crossed_from, first, joined, sc, *refs):
    refs = list(refs)
    take = lambda n: [refs.pop(0) for _ in range(n)]
    toks = take(2)
    weights = (take(len(held_from)), take(len(crossed_from)))
    given = None if first else (take(2), take(2))
    low_ref, second_ref = take(2) if first else (None, None)
    outs = (take(2), take(1 if joined else 2))
    tvs, wvs, tots = (take(2) for _ in range(3))
    sems, out_sems = refs
    deep, half = weights[0][-1].shape
    outer, plane = sc[8], sc[9]
    made, saved = [], []
    first_column = lambda side: pl.multiple_of((1 - plane if side else plane) * half, half)

    def load(src, dst):
        c = pltpu.make_async_copy(src, dst, sems.at[len(made)])
        c.start()
        made.append(c)
        return c

    columns = lambda i: pl.ds(pl.multiple_of((2 * sc[i] + outer) * deep, deep), deep)
    need = {}
    for k in range(2):
        for side, sources in enumerate((held_from, crossed_from)):
            todo = need[k, side] = []
            for i, at in enumerate(sources):
                part = slice(i * deep, (i + 1) * deep)
                if k == 0:
                    w = weights[side][i]
                    if w.shape[1] != half:
                        w = w.at[:, pl.ds(first_column(side), half)]
                    todo.append(load(w, wvs[side].at[part, :]))
                todo.append(load(toks[k].at[:, columns(at)], tvs[side].at[k, :, part]))
            if not first:
                todo.append(load(given[k][side], tots[side].at[k]))

    def start(k, side):
        if not first:
            return tots[side][k]
        if k:
            return 0.0
        return ADAPTER_SCALE * lax.dot_general(
            low_ref[...], second_ref[pl.ds(first_column(side), half), :], (((1,), (1,)), ((), ())),
            preferred_element_type=jnp.float32,
        )

    for k in range(2):
        for side in range(2):
            for c in need[k, side]:
                c.wait()
            tots[side][k] = start(k, side) + jnp.dot(
                tvs[side][k], wvs[side][...], preferred_element_type=jnp.float32
            )
            if k and joined:
                dst = outs[1][0].at[:, side * half : (side + 1) * half]
            else:
                dst = outs[k][side]
            c = pltpu.make_async_copy(tots[side].at[k], dst, out_sems.at[2 * k + side])
            c.start()
            saved.append(c)
    for c in saved:
        c.wait()


def rope_blocks(pos, count, tab_ref, tokens, write):
    starts = SEQ // BLK
    for b in range(tokens // BLK):
        at = pos[b * BLK] // BLK
        cosine, sine = block_tables(
            tab_ref, tab_ref[pl.ds(2 * BLK + at, 1), :], tab_ref[pl.ds(2 * BLK + starts + at, 1), :]
        )
        live = jnp.where(b < count[0], 1.0, 0.0).astype(jnp.float32)
        write(slice(b * BLK, (b + 1) * BLK), cosine * live, sine * live)


def rotate_heads(pre, cosine, sine, res, rows):
    for h in range(pre.shape[1] // HEAD):
        cols = slice(h * HEAD, (h + 1) * HEAD)
        x = pre[:, cols]
        res[rows, cols] = (x * cosine + pltpu.roll(x, HEAD // 2, 1) * sine).astype(jnp.bfloat16)


def load_both(sc, tok_ref, nodes, pieces, tv, wv, sems):
    deep = pieces[0].shape[0]
    chunk = 2 * deep
    outer = sc[8]
    copies = []
    for i, node in enumerate(nodes):
        at = pl.multiple_of(sc[node] * chunk, chunk)
        copies.append((tok_ref.at[:, pl.ds(at, chunk)], tv.at[:, i * chunk : (i + 1) * chunk]))
        for core, piece in ((outer, pieces[2 * i]), (1 - outer, pieces[2 * i + 1])):
            copies.append((piece, wv.at[pl.ds(pl.multiple_of(i * chunk + core * deep, deep), deep), :]))
    made = [pltpu.make_async_copy(src, dst, sems.at[i]) for i, (src, dst) in enumerate(copies)]
    for c in made:
        c.start()
    return made


def held_keys_kernel(
    sc, count, pos, tok_ref, mine_h, mine_c, given_ref, y3, y3_other, a3, a3_other, tab_ref,
    keys_ref, total_ref, tv, wv, vh, vc, vg, res, sems,
):
    half = vh.shape[1]
    chunk = tv.shape[1] // 2
    made = load_both(sc, tok_ref, (17, 13), (y3, y3_other, a3, a3_other), tv, wv, sems)
    made += [
        pltpu.make_async_copy(mine_h, vh, sems.at[6]),
        pltpu.make_async_copy(given_ref, vg, sems.at[7]),
        pltpu.make_async_copy(mine_c, vc, sems.at[8]),
    ]
    for c in made[6:]:
        c.start()
    for c in made:
        c.wait()
    vc[...] = (vc[...] + vg[:, half:]) + jnp.dot(
        tv[:, chunk:], wv[chunk:, :], preferred_element_type=jnp.float32
    )
    last = pltpu.make_async_copy(vc, total_ref, sems.at[10])
    last.start()

    def write(at, cosine, sine):
        pre = jnp.dot(tv[at, 0:chunk], wv[0:chunk, :], preferred_element_type=jnp.float32)
        rotate_heads(pre + (vh[at, :] + vg[at, 0:half]), cosine, sine, res, at)

    rope_blocks(pos, count, tab_ref, vh.shape[0], write)
    save = pltpu.make_async_copy(
        res, keys_ref.at[:, pl.ds(pl.multiple_of(sc[9] * half, half), half)], sems.at[9]
    )
    save.start()
    save.wait()
    last.wait()


def more_kernel(sc, tok_ref, total_ref, e1, e1_other, e2, e2_other, out_ref, tv, wv, vc, sems):
    made = load_both(sc, tok_ref, (15, 16), (e1, e1_other, e2, e2_other), tv, wv, sems)
    total = pltpu.make_async_copy(total_ref, vc, sems.at[6])
    total.start()
    for c in made:
        c.wait()
    total.wait()
    vc[...] += jnp.dot(tv[...], wv[...], preferred_element_type=jnp.float32)
    save = pltpu.make_async_copy(vc, out_ref, sems.at[7])
    save.start()
    save.wait()


def crossed_keys_kernel(
    sc, count, pos, tok_ref, total_ref, e3, e3_other, e0, e0_other, tab_ref, keys_ref, out_ref,
    tv, wv, vc, res, sems,
):
    half = vc.shape[1]
    made = load_both(sc, tok_ref, (17, 14), (e3, e3_other, e0, e0_other), tv, wv, sems)
    total = pltpu.make_async_copy(total_ref, vc, sems.at[6])
    total.start()
    for c in made:
        c.wait()
    total.wait()

    def write(at, cosine, sine):
        pre = vc[at, :] + jnp.dot(tv[at, :], wv[...], preferred_element_type=jnp.float32)
        rotate_heads(pre, cosine, sine, res, at)

    rope_blocks(pos, count, tab_ref, vc.shape[0], write)
    save = pltpu.make_async_copy(
        res, out_ref.at[:, pl.ds(pl.multiple_of((1 - sc[9]) * half, half), half)], sems.at[7]
    )
    save.start()
    save.wait()


class Routes:
    def __init__(self, mesh):
        self.groups, self.nodes, self.outers = (mesh.shape[a] for a in ALL)
        self.z = self.nodes // 2
        line = list(range(self.z))
        ring = line[:1] + line[1::2] + line[2::2][::-1]
        self.next = {ring[i]: ring[(i + 1) % self.z] for i in range(self.z)}
        self.prev = {v: k for k, v in self.next.items()}

    def pairs(self, f):
        at = lambda g, z, y, o: (g * self.nodes + 2 * z + y) * self.outers + o
        return [
            (at(g, z, y, o), at(*f(g, z, y, o)))
            for g in range(self.groups)
            for z in range(self.z)
            for y in range(2)
            for o in range(self.outers)
        ]

    def table(self):
        rows = []
        for _, n, o, g in [
            (0, n, o, g) for g in range(self.groups) for n in range(self.nodes) for o in range(self.outers)
        ]:
            z, y = divmod(n, 2)
            slot = [n ^ (((r >> 2) & 1) << 1 | ((r >> 1) & 1) << 2 | (r & 1)) for r in range(8)]
            from_z = [z]
            for _ in range(self.z - 1):
                from_z.append(self.prev[from_z[-1]])
            rows.append(
                slot + [o, g] + [2 * k + y for k in from_z] + [2 * k + 1 - y for k in from_z]
            )
        return np.array(rows, np.int32)


def call(kernel, name, shapes, in_specs, out_specs, scratch, args, grid=(), prefetch=1, aliases=None):
    return pl.pallas_call(
        kernel,
        out_shape=shapes,
        grid_spec=pltpu.PrefetchScalarGridSpec(
            num_scalar_prefetch=prefetch, grid=grid, in_specs=in_specs, out_specs=out_specs,
            scratch_shapes=scratch,
        ),
        compiler_params=pltpu.CompilerParams(vmem_limit_bytes=VMEM_LIMIT),
        cost_estimate=pl.CostEstimate(flops=1000, bytes_accessed=1024, transcendentals=0),
        input_output_aliases=aliases or {},
        name=name,
    )(*args)


def fast_body(
    routes, tokens, frozen_weight, down_adapter, second_adapter_weight, tenant_ids, block_counts, positions, cotangent
):
    bf16, f32 = jnp.bfloat16, jnp.float32
    rows, width = tokens.shape
    deep, kv = frozen_weight.shape
    nodes = routes.nodes
    chunk = 2 * deep
    half = kv // 2
    rank = down_adapter.shape[1]
    plane = lax.axis_index("groups")
    outer = lax.axis_index("outer")
    tab = jnp.asarray(rope_constants())

    send = lambda x, f: lax.ppermute(x, ALL, routes.pairs(f))
    to_core = lambda g, z, y, o: (g, z, y, 1 - o)
    to_x = lambda g, z, y, o: (1 - g, z, y, o)
    to_y = lambda g, z, y, o: (g, z, 1 - y, o)
    to_z = lambda g, z, y, o: (g, routes.next[z], y, o)
    to_z1 = lambda g, z, y, o: (g, z ^ 1, y, o)
    to_z2 = lambda g, z, y, o: (g, z ^ 2, y, o)
    fence = lambda *x: lax.optimization_barrier(x)
    vm = pl.BlockSpec(memory_space=pltpu.VMEM)
    dma = pltpu.SemaphoreType.DMA
    shape = jax.ShapeDtypeStruct

    def product(held, crossed, given=(), adapters=(), joined=False):
        kh, kc = len(held) * deep, len(crossed) * deep
        outs = [shape((rows, half), f32)] * 2
        outs += [shape((rows, kv), f32)] if joined else outs
        return call(
            functools.partial(
                product_kernel, [i for _, i in held], [i for _, i in crossed], not given, joined
            ),
            "products", outs,
            [ANY] * (2 + len(held) + len(crossed) + len(given)) + [vm] * len(adapters), [ANY] * len(outs),
            [
                pltpu.VMEM((2, rows, kh), bf16), pltpu.VMEM((2, rows, kc), bf16),
                pltpu.VMEM((kh, half), bf16), pltpu.VMEM((kc, half), bf16),
                pltpu.VMEM((2, rows, half), f32), pltpu.VMEM((2, rows, half), f32),
                dma((3 * len(held) + 3 * len(crossed) + 4,)), dma((4,)),
            ],
            (sc, tokens, sib_tokens, *[w for w, _ in held], *[w for w, _ in crossed], *given, *adapters),
        )

    z0 = lax.dynamic_slice(frozen_weight, (0, plane * half), (deep, half))
    z0, own_tokens, table = fence(z0, tokens, jnp.asarray(routes.table()))
    sc = lax.dynamic_slice(table, (lax.axis_index(ALL), 0), (1, table.shape[1]))[0]
    z1 = send(z0, to_z)
    y0 = send(z0, to_y)
    sib_tokens = send(own_tokens, to_core)
    slot_rows = chunk // 2 + kv // nodes // 2
    low, own, sib = call(
        gradient_kernel, "adapter_gradients",
        (
            shape((rows, rank), bf16),
            shape((nodes, slot_rows, rank), f32),
            shape((nodes, slot_rows, rank), bf16),
        ),
        [
            pl.BlockSpec((rows, chunk), lambda i, sc, *_: (0, sc[i])),
            pl.BlockSpec((chunk, rank), lambda i, sc, *_: (sc[i], 0)),
            pl.BlockSpec((kv, rank), lambda i, *_: (0, 0)),
            pl.BlockSpec((rows, kv), lambda i, *_: (0, 0)),
            pl.BlockSpec(tab.shape, lambda i, *_: (0, 0)),
        ],
        (
            pl.BlockSpec((rows, rank), lambda i, *_: (0, 0)),
            pl.BlockSpec((nodes, slot_rows, rank), lambda i, *_: (0, 0, 0)),
            pl.BlockSpec((nodes, slot_rows, rank), lambda i, *_: (0, 0, 0)),
        ),
        [
            pltpu.VMEM((rows, kv), bf16),
            pltpu.VMEM((rows, rank), bf16),
            pltpu.VMEM((rows, rank), f32),
            pltpu.VMEM((max(chunk, kv), rank), f32),
        ],
        (sc, tenant_ids, block_counts, positions, tokens, down_adapter, second_adapter_weight, cotangent, tab),
        grid=(nodes,), prefetch=4,
    )
    z1, y0, low, own, sib, sib_tokens = fence(z1, y0, low, own, sib, sib_tokens)

    z2 = send(z1, to_z)
    y1 = send(z1, to_y)
    a1 = send(z1, to_x)
    other = send(sib, to_core)
    totals = product(
        ((frozen_weight, 10), (y0, 14), (z1, 11)), ((frozen_weight, 10),), adapters=(low, second_adapter_weight)
    )
    z2, y1, a1, other, *totals = fence(z2, y1, a1, other, *totals)

    z3 = send(z2, to_z)
    y2 = send(z2, to_y)
    a2 = send(z2, to_x)
    s = own + other.astype(f32)
    totals = product(((y1, 15), (z2, 12)), ((a1, 11),), given=totals)
    z3, y2, a2, s, *totals = fence(z3, y2, a2, s, *totals)

    y3 = send(z3, to_y)
    a3 = send(z3, to_x)
    got = send(s[4:].astype(bf16), to_z1)
    mine_h, mine_c, theirs = product(((y2, 16), (z3, 13)), ((a2, 12),), given=totals, joined=True)
    y3, a3, got, mine_h, mine_c, theirs = fence(y3, a3, got, mine_h, mine_c, theirs)

    given, y3_other, a3_other = send(theirs, to_core), send(y3, to_core), send(a3, to_core)
    e1 = send(y1, to_x)
    e2 = send(a2, to_y)
    s = s[:4] + got.astype(f32)
    got = send(s[2:].astype(bf16), to_z2)
    own_space = [
        pltpu.VMEM((rows, 2 * chunk), bf16), pltpu.VMEM((2 * chunk, half), bf16), pltpu.VMEM((rows, half), f32),
    ]
    keys, total = call(
        held_keys_kernel, "held_keys", [shape((rows, kv), bf16), shape((rows, half), f32)],
        [ANY] * 8 + [vm], [ANY, ANY],
        own_space + [
            pltpu.VMEM((rows, half), f32), pltpu.VMEM((rows, kv), f32), pltpu.VMEM((rows, half), bf16), dma((11,)),
        ],
        (sc, block_counts, positions, tokens, mine_h, mine_c, given, y3, y3_other, a3, a3_other, tab),
        prefetch=3,
    )
    y3, weight, total = fence(y3, frozen_weight, total)
    e3 = send(y3, to_x)
    e0 = send(lax.dynamic_slice(weight, (0, (1 - plane) * half), (deep, half)), to_y)
    e1, e2, got, total = fence(e1, e2, got, total)

    s = s[:2] + got.astype(f32)
    got = send(s[1].astype(bf16), to_y)
    total = call(
        more_kernel, "more_products", shape((rows, half), f32), [ANY] * 6, ANY, own_space + [dma((8,))],
        (sc, tokens, total, e1, send(e1, to_core), e2, send(e2, to_core)),
    )
    e3, e0, got, total = fence(e3, e0, got, total)

    s = s[0] + got.astype(f32)
    t = send(s, to_core)
    keys = call(
        crossed_keys_kernel, "crossed_keys", shape((rows, kv), bf16), [ANY] * 6 + [vm, ANY], ANY,
        own_space + [pltpu.VMEM((rows, half), bf16), dma((8,))],
        (sc, block_counts, positions, tokens, total, e3, send(e3, to_core), e0, send(e0, to_core), tab, keys),
        prefetch=3, aliases={10: 0},
    )
    down_rows = chunk // 2
    lower, upper = jnp.where(outer == 0, s, t), jnp.where(outer == 0, t, s)
    down = jnp.concatenate((lower[:down_rows], upper[:down_rows]))
    up = jnp.concatenate((lower[down_rows:], upper[down_rows:]))
    return keys, down, up


def rope_tables(positions):
    half_head = HEAD // 2
    frequency = ROPE_BASE ** (-2.0 * jnp.arange(half_head, dtype=jnp.float32) / HEAD)
    angle = positions.astype(jnp.float32)[:, None] * frequency[None, :]
    return (jnp.cos(angle), jnp.sin(angle))


def rotate(field, cosine, sine, orient):
    rows = field.shape[0]
    shaped = field.reshape(rows, -1, 2, HEAD // 2)
    first = shaped[:, :, 0]
    second = shaped[:, :, 1]
    cos_b = cosine[:, None, :]
    sin_b = orient * sine[:, None, :]
    out_first = first * cos_b - second * sin_b
    out_second = second * cos_b + first * sin_b
    return jnp.stack((out_first, out_second), axis=2).reshape(rows, -1)


def plain_body(
    tokens, frozen_weight, down_adapter, second_adapter_weight, tenant_ids, block_counts, positions, cotangent
):
    token_rows = tokens.shape[0]
    block_total = tenant_ids.shape[0]
    block_rows = token_rows // block_total
    width_cols = down_adapter.shape[1]
    live_blocks = (jnp.arange(block_total, dtype=jnp.int32) < block_counts[0]).astype(jnp.float32)
    live_rows = jnp.repeat(live_blocks, block_rows)[:, None]
    column_tenant = jnp.arange(width_cols, dtype=jnp.int32) // R
    select_blocks = (tenant_ids[:, None] == column_tenant[None, :]).astype(
        jnp.float32
    ) * live_blocks[:, None]
    select = jnp.repeat(select_blocks, block_rows, axis=0)
    lowrank_hidden = (
        jnp.dot(tokens, down_adapter, preferred_element_type=jnp.float32) * select
    ).astype(jnp.bfloat16)
    frozen_output = jnp.dot(
        tokens,
        lax.all_gather(frozen_weight, ("node", "outer"), axis=0, tiled=True),
        preferred_element_type=jnp.float32,
    )
    adapter_output = lax.dot_general(
        lowrank_hidden,
        second_adapter_weight,
        (((1,), (1,)), ((), ())),
        preferred_element_type=jnp.float32,
    )
    unrotated_keys = frozen_output + ADAPTER_SCALE * adapter_output
    cosine, sine = rope_tables(positions)
    keys = (live_rows * rotate(unrotated_keys, cosine, sine, 1.0)).astype(jnp.bfloat16)
    output_gradient = (
        live_rows * rotate(cotangent.astype(jnp.float32), cosine, sine, -1.0)
    ).astype(jnp.bfloat16)
    backward_gradient = (
        jnp.dot(output_gradient, second_adapter_weight, preferred_element_type=jnp.float32) * select
    ).astype(jnp.bfloat16)
    down_product = ADAPTER_SCALE * lax.dot_general(
        tokens, backward_gradient, (((0,), (0,)), ((), ())), preferred_element_type=jnp.float32
    )
    up_product = ADAPTER_SCALE * lax.dot_general(
        output_gradient,
        lowrank_hidden,
        (((0,), (0,)), ((), ())),
        preferred_element_type=jnp.float32,
    )
    shares = (
        lax.psum_scatter(down_product, "node", scatter_dimension=0, tiled=True),
        lax.psum_scatter(up_product, "node", scatter_dimension=0, tiled=True),
    )
    down_adapter_gradient, up_adapter_gradient = lax.psum((shares[0], shares[1]), "outer")
    return (keys, down_adapter_gradient, up_adapter_gradient)


def solution(mesh):
    placed = (
        P(("groups", "node", "outer"), None),
        P(("node", "outer"), None),
        P(),
        P(),
        P(("groups", "node", "outer")),
        P(("groups", "node", "outer")),
        P(("groups", "node", "outer")),
        P(("groups", "node", "outer"), None),
    )
    routed = tuple(mesh.shape[a] for a in ALL) == (2, 8, 2)
    return jax.shard_map(
        functools.partial(fast_body, Routes(mesh)) if routed else plain_body,
        mesh=mesh,
        in_specs=placed,
        out_specs=(
            P(("groups", "node", "outer"), None),
            P(("groups", "node"), None),
            P(("groups", "node"), None),
        ),
        check_vma=False,
    )
```

```python
import functools

import jax
import jax.numpy as jnp
import numpy as np
from jax import lax
from jax.experimental import pallas as pl
from jax.experimental.pallas import tpu as pltpu
from jax.sharding import PartitionSpec as P

HEAD = 128
R = 16
BLK = 128
SEQ = 4096
ROPE_BASE = 500000.0
ADAPTER_SCALE = 2.0
ALL = ("groups", "node", "outer")
HBM = pl.BlockSpec(memory_space=pltpu.HBM)
ANY = pl.BlockSpec(memory_space=pl.ANY)
MIB = 1024 * 1024


def rope_constants():
    half = HEAD // 2
    frequency = ROPE_BASE ** (-2.0 * np.arange(half) / HEAD)
    inside = np.arange(BLK)[:, None] * frequency[None, :]
    starts = BLK * np.arange(SEQ // BLK)[:, None] * frequency[None, :]
    both = lambda t: np.concatenate((t, t), axis=1)
    return np.concatenate(
        (both(np.cos(inside)), both(np.sin(inside)), both(np.cos(starts)), both(np.sin(starts)))
    ).astype(np.float32)


def block_tables(tab_ref, c_row, s_row):
    c_in = tab_ref[0:BLK, :]
    s_in = tab_ref[BLK : 2 * BLK, :]
    cosine = c_in * c_row - s_in * s_row
    sine = s_in * c_row + c_in * s_row
    lane = lax.broadcasted_iota(jnp.int32, (1, HEAD), 1)
    return cosine, jnp.where(lane < HEAD // 2, -sine, sine)


def gradient_kernel(
    sc, tids, count, pos, tok_ref, a_ref, b_ref, cot_ref, tab_ref, low_ref, own_ref, sib_ref,
    tv, av, bv, cv, tab, cosines, sines, grad, low, back, piece, sems,
):
    slots, rows, chunk = tv.shape
    down_half, up_half = chunk // 2, HEAD // 2
    outer = sc[8]
    lane = lax.broadcasted_iota(jnp.int32, (1, HEAD), 1)

    def chunk_copies(i):
        columns = pl.ds(pl.multiple_of(sc[i] * chunk, chunk), chunk)
        heads = pl.ds(pl.multiple_of(i * HEAD, HEAD), HEAD)
        return (
            pltpu.make_async_copy(cot_ref.at[:, heads], cv.at[i], sems.at[0, i]),
            pltpu.make_async_copy(a_ref.at[columns, :], av.at[i], sems.at[1, i]),
            pltpu.make_async_copy(tok_ref.at[:, columns], tv.at[i], sems.at[2, i]),
        )

    small = (
        pltpu.make_async_copy(tab_ref, tab, sems.at[3, 0]), pltpu.make_async_copy(b_ref, bv, sems.at[3, 1]),
    )
    for c in small:
        c.start()
    for i in range(slots):
        for c in chunk_copies(i):
            c.start()
    for c in small:
        c.wait()

    def keep_tables(at, cosine, sine):
        cosines[at, :] = cosine
        sines[at, :] = sine

    rope_blocks(pos, count, tab, rows, keep_tables)
    low[...] = jnp.zeros_like(low)
    back[...] = jnp.zeros_like(back)

    @pl.loop(0, slots)
    def _(i):
        for c in chunk_copies(i):
            c.wait()
        low[...] += jnp.dot(tv[i], av[i], preferred_element_type=jnp.float32)
        x = cv[i].astype(jnp.float32)
        g = (x * cosines[...] - pltpu.roll(x, HEAD // 2, 1) * sines[...]).astype(jnp.bfloat16)
        grad[i] = g
        second = bv[pl.ds(pl.multiple_of(i * HEAD, HEAD), HEAD), :]
        back[...] += jnp.dot(g, second, preferred_element_type=jnp.float32)

    for b in range(rows // BLK):
        at = slice(b * BLK, (b + 1) * BLK)
        hit = jnp.logical_and(lane // R == tids[b], b < count[0])
        select = jnp.where(hit, 1.0, 0.0).astype(jnp.float32)
        low_ref[at, :] = (low[at, :] * select).astype(jnp.bfloat16)
        back[at, :] = ADAPTER_SCALE * (back[at, :] * select).astype(jnp.bfloat16).astype(jnp.float32)
    turned = back[...].astype(jnp.bfloat16)
    contract = (((0,), (0,)), ((), ()))

    @pl.loop(0, slots)
    def _(i):
        for core, out in ((outer, own_ref), (1 - outer, sib_ref)):
            columns = pl.ds(pl.multiple_of(core * down_half, down_half), down_half)
            down = lax.dot_general(turned, tv[i, :, columns], contract, preferred_element_type=jnp.float32)
            out[i, 0:down_half, :] = down.T.astype(out.dtype)
        piece[...] = ADAPTER_SCALE * lax.dot_general(
            grad[sc[i]], low_ref[...], contract, preferred_element_type=jnp.float32
        )
        for core, out in ((outer, own_ref), (1 - outer, sib_ref)):
            at = pl.multiple_of(core * up_half, up_half)
            out[i, down_half:, :] = piece[pl.ds(at, up_half), :].astype(out.dtype)


def product_kernel(held_from, crossed_from, first, joined, sc, *refs):
    refs = list(refs)
    take = lambda n: [refs.pop(0) for _ in range(n)]
    toks = take(2)
    weights = (take(len(held_from)), take(len(crossed_from)))
    given = None if first else (take(2), take(2))
    low_ref, second_ref = take(2) if first else (None, None)
    outs = (take(2), take(1 if joined else 2))
    spare = take(1) if first else []
    tvs, wvs, tots = (take(2) for _ in range(3))
    sems, out_sems = refs
    deep, half = weights[0][-1].shape
    outer, plane = sc[8], sc[9]
    made, saved = [], []
    first_column = lambda side: pl.multiple_of((1 - plane if side else plane) * half, half)

    def load(src, dst):
        c = pltpu.make_async_copy(src, dst, sems.at[len(made)])
        c.start()
        made.append(c)
        return c

    columns = lambda i: pl.ds(pl.multiple_of((2 * sc[i] + outer) * deep, deep), deep)
    need = {}
    for k in range(2):
        for side, sources in enumerate((held_from, crossed_from)):
            todo = need[k, side] = []
            for i, at in enumerate(sources):
                part = slice(i * deep, (i + 1) * deep)
                if k == 0:
                    w = weights[side][i]
                    if w.shape[1] != half:
                        w = w.at[:, pl.ds(first_column(side), half)]
                    todo.append(load(w, wvs[side].at[part, :]))
                todo.append(load(toks[k].at[:, columns(at)], tvs[side].at[k, :, part]))
            if not first:
                todo.append(load(given[k][side], tots[side].at[k]))

    def start(k, side):
        if not first:
            return tots[side][k]
        if k:
            return 0.0
        return ADAPTER_SCALE * lax.dot_general(
            low_ref[...], second_ref[pl.ds(first_column(side), half), :], (((1,), (1,)), ((), ())),
            preferred_element_type=jnp.float32,
        )

    for k in range(2):
        for side in range(2):
            for c in need[k, side]:
                c.wait()
            if first and k == 0 and side:
                c = pltpu.make_async_copy(wvs[1].at[0:deep, :], spare[0], out_sems.at[4])
                c.start()
                saved.append(c)
            tots[side][k] = start(k, side) + jnp.dot(
                tvs[side][k], wvs[side][...], preferred_element_type=jnp.float32
            )
            if k and joined:
                dst = outs[1][0].at[:, side * half : (side + 1) * half]
            else:
                dst = outs[k][side]
            c = pltpu.make_async_copy(tots[side].at[k], dst, out_sems.at[2 * k + side])
            c.start()
            saved.append(c)
    for c in saved:
        c.wait()


def rope_blocks(pos, count, tab_ref, tokens, write):
    starts = SEQ // BLK
    for b in range(tokens // BLK):
        at = pos[b * BLK] // BLK
        cosine, sine = block_tables(
            tab_ref, tab_ref[pl.ds(2 * BLK + at, 1), :], tab_ref[pl.ds(2 * BLK + starts + at, 1), :]
        )
        live = jnp.where(b < count[0], 1.0, 0.0).astype(jnp.float32)
        write(slice(b * BLK, (b + 1) * BLK), cosine * live, sine * live)


def rotate_heads(pre, cosine, sine, res, rows):
    for h in range(pre.shape[1] // HEAD):
        cols = slice(h * HEAD, (h + 1) * HEAD)
        x = pre[:, cols]
        res[rows, cols] = (x * cosine + pltpu.roll(x, HEAD // 2, 1) * sine).astype(jnp.bfloat16)


def load_tokens(sc, tok_ref, nodes, pieces, tv, wv, sems):
    deep = pieces[0].shape[0]
    outer, copies = sc[8], []
    for core in range(2):
        for i, node in enumerate(nodes):
            at = pl.multiple_of((2 * sc[node] + (1 - outer if core else outer)) * deep, deep)
            to = (core * len(nodes) + i) * deep
            copies.append((tok_ref.at[:, pl.ds(at, deep)], tv.at[:, to : to + deep]))
            if not core:
                copies.append((pieces[i], wv.at[i * deep : (i + 1) * deep, :]))
    made = [pltpu.make_async_copy(src, dst, sems.at[i]) for i, (src, dst) in enumerate(copies)]
    for c in made:
        c.start()
    return made


def dots(tok, columns, weights):
    total = None
    for at, w in zip(columns, weights):
        part = jnp.dot(tok[:, at : at + w.shape[0]], w[...], preferred_element_type=jnp.float32)
        total = part if total is None else total + part
    return total


def held_keys_kernel(
    sc, count, pos, tok_ref, mine_h, mine_c, y3, a3, given, y3_other, a3_other, tab_ref,
    keys_ref, total_ref, tv, wv, vh, vc, res, sems,
):
    deep, half = y3.shape
    made = load_tokens(sc, tok_ref, (17, 13), (y3, a3), tv, wv, sems)
    made += [pltpu.make_async_copy(mine_h, vh, sems.at[6]), pltpu.make_async_copy(mine_c, vc, sems.at[7])]
    for c in made[6:]:
        c.start()
    for c in made:
        c.wait()
    vc[...] = (vc[...] + given[:, half:]) + dots(tv, (deep, 3 * deep), (wv.at[deep : 2 * deep, :], a3_other))
    last = pltpu.make_async_copy(vc, total_ref, sems.at[8])
    last.start()

    def write(at, cosine, sine):
        pre = dots(tv.at[at, :], (0, 2 * deep), (wv.at[0:deep, :], y3_other))
        rotate_heads(pre + (vh[at, :] + given[at, 0:half]), cosine, sine, res, at)

    rope_blocks(pos, count, tab_ref, vh.shape[0], write)
    save = pltpu.make_async_copy(
        res, keys_ref.at[:, pl.ds(pl.multiple_of(sc[9] * half, half), half)], sems.at[9]
    )
    save.start()
    save.wait()
    last.wait()


def crossed_kernel(sc, tok_ref, sib_ref, total_ref, e1, e2, mine_ref, theirs_ref, tv, wv, vc, sems, out_sems):
    deep = e1.shape[0]
    outer, copies = sc[8], []
    for i, (node, piece) in enumerate(((15, e1), (16, e2))):
        part = slice(i * deep, (i + 1) * deep)
        at = pl.multiple_of((2 * sc[node] + outer) * deep, deep)
        copies.append((piece, wv.at[part, :]))
        for k, tok in enumerate((tok_ref, sib_ref)):
            copies.append((tok.at[:, pl.ds(at, deep)], tv.at[k, :, part]))
    copies.append((total_ref, vc.at[0]))
    made = [pltpu.make_async_copy(src, dst, sems.at[i]) for i, (src, dst) in enumerate(copies)]
    for c in made:
        c.start()
    for c in made:
        c.wait()
    saves = []
    for k, dst in enumerate((mine_ref, theirs_ref)):
        part = jnp.dot(tv[k], wv[...], preferred_element_type=jnp.float32)
        vc[k] = part if k else vc[0] + part
        saves.append(pltpu.make_async_copy(vc.at[k], dst, out_sems.at[k]))
        saves[-1].start()
    for c in saves:
        c.wait()


def fold_kernel(keep_ref, got_ref, next_ref, *send_refs):
    at = next_ref.shape[0]
    next_ref[...] = keep_ref[0:at] + got_ref[0:at].astype(jnp.float32)
    for ref in send_refs:
        n = ref.shape[0]
        ref[...] = (keep_ref[at : at + n] + got_ref[at : at + n].astype(jnp.float32)).astype(ref.dtype)
        at += n


def sum_kernel(keep_ref, *refs):
    total = keep_ref[...]
    for ref in refs[:-1]:
        total = total + ref[...].astype(jnp.float32)
    refs[-1][...] = total


def crossed_keys_kernel(
    sc, count, pos, tok_ref, total_ref, e3, e0, e3_other, e0_other, given, share, share_other, tab_ref,
    keys_ref, out_ref, down_ref, up_ref, tv, wv, vc, res, sems,
):
    deep, half = e3.shape
    outer = sc[8]
    down_rows = down_ref.shape[0] // 2
    up_rows = up_ref.shape[0] // 2
    made = load_tokens(sc, tok_ref, (17, 14), (e3, e0), tv, wv, sems)
    total = pltpu.make_async_copy(total_ref, vc, sems.at[6])
    total.start()
    saves = []
    for i, (core, sums) in enumerate(((outer, share), (1 - outer, share_other))):
        down_at = pl.multiple_of(core * down_rows, down_rows)
        up_at = pl.multiple_of(core * up_rows, up_rows)
        saves += [
            pltpu.make_async_copy(
                sums.at[0, 0:down_rows, :], down_ref.at[pl.ds(down_at, down_rows), :], sems.at[7 + 2 * i]
            ),
            pltpu.make_async_copy(
                sums.at[0, down_rows:, :], up_ref.at[pl.ds(up_at, up_rows), :], sems.at[8 + 2 * i]
            ),
        ]
    for c in saves:
        c.start()
    for c in made:
        c.wait()
    total.wait()

    def write(at, cosine, sine):
        pre = vc[at, :] + given[at, :] + dots(tv.at[at, :], (0, 2 * deep, 3 * deep), (wv, e3_other, e0_other))
        rotate_heads(pre, cosine, sine, res, at)

    rope_blocks(pos, count, tab_ref, vc.shape[0], write)
    saves.append(
        pltpu.make_async_copy(
            res, out_ref.at[:, pl.ds(pl.multiple_of((1 - sc[9]) * half, half), half)], sems.at[11]
        )
    )
    saves[-1].start()
    for c in saves:
        c.wait()


class Routes:
    def __init__(self, mesh):
        self.groups, self.nodes, self.outers = (mesh.shape[a] for a in ALL)
        self.z = self.nodes // 2
        line = list(range(self.z))
        ring = line[:1] + line[1::2] + line[2::2][::-1]
        self.next = {ring[i]: ring[(i + 1) % self.z] for i in range(self.z)}
        self.prev = {v: k for k, v in self.next.items()}

    def pairs(self, f):
        at = lambda g, z, y, o: (g * self.nodes + 2 * z + y) * self.outers + o
        return [
            (at(g, z, y, o), at(*f(g, z, y, o)))
            for g in range(self.groups)
            for z in range(self.z)
            for y in range(2)
            for o in range(self.outers)
        ]

    def table(self):
        rows = []
        for _, n, o, g in [
            (0, n, o, g) for g in range(self.groups) for n in range(self.nodes) for o in range(self.outers)
        ]:
            z, y = divmod(n, 2)
            slot = [n ^ ((r >> 2) & 1 | ((r >> 1) & 1) << 1 | (r & 1) << 2) for r in range(8)]
            from_z = [z]
            for _ in range(self.z - 1):
                from_z.append(self.prev[from_z[-1]])
            rows.append(
                slot + [o, g] + [2 * k + y for k in from_z] + [2 * k + 1 - y for k in from_z]
            )
        return np.array(rows, np.int32)


def call(kernel, name, shapes, in_specs, out_specs, scratch, args, grid=(), prefetch=1, aliases=None, vmem=16):
    specs = [None] * prefetch + in_specs
    return pl.pallas_call(
        kernel,
        out_shape=shapes,
        grid_spec=pltpu.PrefetchScalarGridSpec(
            num_scalar_prefetch=prefetch, grid=grid, in_specs=in_specs, out_specs=out_specs,
            scratch_shapes=scratch,
        ),
        compiler_params=pltpu.CompilerParams(vmem_limit_bytes=vmem * MIB),
        cost_estimate=pl.CostEstimate(flops=1000, bytes_accessed=1024, transcendentals=0),
        input_output_aliases=aliases or {},
        name=name,
    )(*[pltpu.with_memory_space_constraint(x, pltpu.HBM) if spec is HBM else x for x, spec in zip(args, specs)])


def fast_body(
    routes, tokens, frozen_weight, down_adapter, second_adapter_weight, tenant_ids, block_counts, positions, cotangent
):
    bf16, f32 = jnp.bfloat16, jnp.float32
    rows, width = tokens.shape
    deep, kv = frozen_weight.shape
    nodes = routes.nodes
    chunk = 2 * deep
    half = kv // 2
    rank = down_adapter.shape[1]
    plane = lax.axis_index("groups")
    outer = lax.axis_index("outer")
    tab = jnp.asarray(rope_constants())

    send = lambda x, f: lax.ppermute(x, ALL, routes.pairs(f))
    to_core = lambda g, z, y, o: (g, z, y, 1 - o)
    to_x = lambda g, z, y, o: (1 - g, z, y, o)
    to_y = lambda g, z, y, o: (g, z, 1 - y, o)
    to_z = lambda g, z, y, o: (g, routes.next[z], y, o)
    to_z1 = lambda g, z, y, o: (g, z ^ 1, y, o)
    to_z2 = lambda g, z, y, o: (g, z ^ 2, y, o)
    to_z3 = lambda g, z, y, o: (g, z ^ 3, y, o)
    fence = lambda *x: lax.optimization_barrier(x)
    vm = pl.BlockSpec(memory_space=pltpu.VMEM)
    dma = pltpu.SemaphoreType.DMA
    shape = jax.ShapeDtypeStruct

    def fold(keep, got, stay, *go):
        slots = lambda n, dtype: pltpu.VMEM((n, *keep.shape[1:]), dtype)
        return call(
            fold_kernel, "fold", [slots(stay, f32), *[slots(n, bf16) for n in go]],
            [vm, vm], [vm] * (1 + len(go)), [], (keep, got), prefetch=0,
        )

    def product(held, crossed, given=(), adapters=(), joined=False):
        kh, kc = len(held) * deep, len(crossed) * deep
        outs = [pltpu.VMEM((rows, half), f32)] * 2
        outs += [pltpu.VMEM((rows, kv), f32)] if joined else outs
        outs += [] if given else [shape((deep, half), bf16)]
        return call(
            functools.partial(
                product_kernel, [i for _, i in held], [i for _, i in crossed], not given, joined
            ),
            "products", outs,
            [HBM] * 2 + [HBM if w is frozen_weight else ANY for w, _ in held + crossed] + [ANY] * len(given)
            + [vm] * len(adapters), [ANY] * len(outs),
            [
                pltpu.VMEM((2, rows, kh), bf16), pltpu.VMEM((2, rows, kc), bf16),
                pltpu.VMEM((kh, half), bf16), pltpu.VMEM((kc, half), bf16),
                pltpu.VMEM((2, rows, half), f32), pltpu.VMEM((2, rows, half), f32),
                dma((3 * len(held) + 3 * len(crossed) + 4,)), dma((5,)),
            ],
            (sc, tokens, sib_tokens, *[w for w, _ in held], *[w for w, _ in crossed], *given, *adapters),
        )

    z0 = lax.dynamic_slice(frozen_weight, (0, plane * half), (deep, half))
    z0, own_tokens, table = fence(z0, tokens, jnp.asarray(routes.table()))
    sc = lax.dynamic_slice(table, (lax.axis_index(ALL), 0), (1, table.shape[1]))[0]
    z1 = send(z0, to_z)
    y0 = send(z0, to_y)
    sib_tokens = send(own_tokens, to_core)
    slot_rows = chunk // 2 + kv // nodes // 2
    low, own, sib = call(
        gradient_kernel, "adapter_gradients",
        [
            pltpu.VMEM((rows, rank), bf16), pltpu.VMEM((nodes, slot_rows, rank), f32),
            pltpu.VMEM((nodes, slot_rows, rank), bf16),
        ],
        [HBM] * 5, [vm] * 3,
        [
            pltpu.VMEM((nodes, rows, chunk), bf16), pltpu.VMEM((nodes, chunk, rank), bf16),
            pltpu.VMEM((kv, rank), bf16), pltpu.VMEM((nodes, rows, HEAD), bf16), pltpu.VMEM(tab.shape, f32),
            pltpu.VMEM((rows, HEAD), f32), pltpu.VMEM((rows, HEAD), f32), pltpu.VMEM((nodes, rows, HEAD), bf16),
            pltpu.VMEM((rows, rank), f32), pltpu.VMEM((rows, rank), f32), pltpu.VMEM((HEAD, rank), f32),
            dma((4, nodes)),
        ],
        (sc, tenant_ids, block_counts, positions, tokens, down_adapter, second_adapter_weight, cotangent, tab),
        prefetch=4, vmem=52,
    )
    z1, y0, low, own, sib, sib_tokens = fence(z1, y0, low, own, sib, sib_tokens)

    z2 = send(z1, to_z)
    y1 = send(z1, to_y)
    a1 = send(z1, to_x)
    other = send(sib, to_core)
    *totals, c0 = product(
        ((frozen_weight, 10), (y0, 14), (z1, 11)), ((frozen_weight, 10),), adapters=(low, second_adapter_weight)
    )
    z2, y1, a1, other, *totals = fence(z2, y1, a1, other, *totals)

    z3 = send(z2, to_z)
    y2 = send(z2, to_y)
    a2 = send(z2, to_x)
    keep, out = fold(own, other, 4, 4)
    totals = product(((y1, 15), (z2, 12)), ((a1, 11),), given=totals)
    z3, y2, a2, keep, out, *totals = fence(z3, y2, a2, keep, out, *totals)

    y3 = send(y2, to_z)
    a3 = send(z3, to_x)
    got = send(out, to_y)
    mine_h, mine_c, theirs = product(((y2, 16), (z3, 13)), ((a2, 12),), given=totals, joined=True)
    y3, a3, got, mine_h, mine_c, theirs = fence(y3, a3, got, mine_h, mine_c, theirs)

    given, y3_other, a3_other = send(theirs, to_core), send(y3, to_core), send(a3, to_core)
    e1 = send(y1, to_x)
    e2 = send(a2, to_y)
    keep, *out = fold(keep, got, 1, 1, 1, 1)
    got = [send(x, f) for x, f in zip(out, (to_z2, to_z1, to_z3))]
    own_space = [
        pltpu.VMEM((rows, 2 * chunk), bf16), pltpu.VMEM((chunk, half), bf16), pltpu.VMEM((rows, half), f32),
    ]
    keys, total = call(
        held_keys_kernel, "held_keys", [shape((rows, kv), bf16), pltpu.VMEM((rows, half), f32)],
        [HBM] + [ANY] * 4 + [vm] * 4, [ANY, ANY],
        own_space + [pltpu.VMEM((rows, half), f32), pltpu.VMEM((rows, half), bf16), dma((10,))],
        (sc, block_counts, positions, tokens, mine_h, mine_c, y3, a3, given, y3_other, a3_other, tab),
        prefetch=3,
    )
    y3, c0, total = fence(y3, c0, total)
    e3 = send(y3, to_x)
    e0 = send(c0, to_y)
    e1, e2, total = fence(e1, e2, total)
    mine, theirs = call(
        crossed_kernel, "crossed_products", [pltpu.VMEM((rows, half), f32)] * 2,
        [HBM] * 2 + [ANY] * 3, [ANY, ANY],
        [
            pltpu.VMEM((2, rows, chunk), bf16), pltpu.VMEM((chunk, half), bf16),
            pltpu.VMEM((2, rows, half), f32), dma((7,)), dma((2,)),
        ],
        (sc, tokens, sib_tokens, total, e1, e2),
    )
    e3, e0, mine, theirs, *got = fence(e3, e0, mine, theirs, *got)

    share = call(
        sum_kernel, "share", pltpu.VMEM(keep.shape, f32), [vm] * 4, vm, [], (keep, *got), prefetch=0,
    )
    keys, down, up = call(
        crossed_keys_kernel, "crossed_keys",
        [shape((rows, kv), bf16), shape((chunk, rank), f32), shape((kv // nodes, rank), f32)],
        [HBM] + [ANY] * 3 + [vm] * 6 + [ANY], [ANY] * 3,
        own_space + [pltpu.VMEM((rows, half), bf16), dma((12,))],
        (
            sc, block_counts, positions, tokens, mine, e3, e0, send(e3, to_core), send(e0, to_core),
            send(theirs, to_core), share, send(share, to_core), tab, keys,
        ),
        prefetch=3, aliases={13: 0},
    )
    return keys, down, up


def rope_tables(positions):
    half_head = HEAD // 2
    frequency = ROPE_BASE ** (-2.0 * jnp.arange(half_head, dtype=jnp.float32) / HEAD)
    angle = positions.astype(jnp.float32)[:, None] * frequency[None, :]
    return (jnp.cos(angle), jnp.sin(angle))


def rotate(field, cosine, sine, orient):
    rows = field.shape[0]
    shaped = field.reshape(rows, -1, 2, HEAD // 2)
    first = shaped[:, :, 0]
    second = shaped[:, :, 1]
    cos_b = cosine[:, None, :]
    sin_b = orient * sine[:, None, :]
    out_first = first * cos_b - second * sin_b
    out_second = second * cos_b + first * sin_b
    return jnp.stack((out_first, out_second), axis=2).reshape(rows, -1)


def plain_body(
    tokens, frozen_weight, down_adapter, second_adapter_weight, tenant_ids, block_counts, positions, cotangent
):
    token_rows = tokens.shape[0]
    block_total = tenant_ids.shape[0]
    block_rows = token_rows // block_total
    width_cols = down_adapter.shape[1]
    live_blocks = (jnp.arange(block_total, dtype=jnp.int32) < block_counts[0]).astype(jnp.float32)
    live_rows = jnp.repeat(live_blocks, block_rows)[:, None]
    column_tenant = jnp.arange(width_cols, dtype=jnp.int32) // R
    select_blocks = (tenant_ids[:, None] == column_tenant[None, :]).astype(
        jnp.float32
    ) * live_blocks[:, None]
    select = jnp.repeat(select_blocks, block_rows, axis=0)
    lowrank_hidden = (
        jnp.dot(tokens, down_adapter, preferred_element_type=jnp.float32) * select
    ).astype(jnp.bfloat16)
    frozen_output = jnp.dot(
        tokens,
        lax.all_gather(frozen_weight, ("node", "outer"), axis=0, tiled=True),
        preferred_element_type=jnp.float32,
    )
    adapter_output = lax.dot_general(
        lowrank_hidden,
        second_adapter_weight,
        (((1,), (1,)), ((), ())),
        preferred_element_type=jnp.float32,
    )
    unrotated_keys = frozen_output + ADAPTER_SCALE * adapter_output
    cosine, sine = rope_tables(positions)
    keys = (live_rows * rotate(unrotated_keys, cosine, sine, 1.0)).astype(jnp.bfloat16)
    output_gradient = (
        live_rows * rotate(cotangent.astype(jnp.float32), cosine, sine, -1.0)
    ).astype(jnp.bfloat16)
    backward_gradient = (
        jnp.dot(output_gradient, second_adapter_weight, preferred_element_type=jnp.float32) * select
    ).astype(jnp.bfloat16)
    down_product = ADAPTER_SCALE * lax.dot_general(
        tokens, backward_gradient, (((0,), (0,)), ((), ())), preferred_element_type=jnp.float32
    )
    up_product = ADAPTER_SCALE * lax.dot_general(
        output_gradient,
        lowrank_hidden,
        (((0,), (0,)), ((), ())),
        preferred_element_type=jnp.float32,
    )
    shares = (
        lax.psum_scatter(down_product, "node", scatter_dimension=0, tiled=True),
        lax.psum_scatter(up_product, "node", scatter_dimension=0, tiled=True),
    )
    down_adapter_gradient, up_adapter_gradient = lax.psum((shares[0], shares[1]), "outer")
    return (keys, down_adapter_gradient, up_adapter_gradient)


def solution(mesh):
    placed = (
        P(("groups", "node", "outer"), None),
        P(("node", "outer"), None),
        P(),
        P(),
        P(("groups", "node", "outer")),
        P(("groups", "node", "outer")),
        P(("groups", "node", "outer")),
        P(("groups", "node", "outer"), None),
    )
    routed = tuple(mesh.shape[a] for a in ALL) == (2, 8, 2)
    return jax.shard_map(
        functools.partial(fast_body, Routes(mesh)) if routed else plain_body,
        mesh=mesh,
        in_specs=placed,
        out_specs=(
            P(("groups", "node", "outer"), None),
            P(("groups", "node"), None),
            P(("groups", "node"), None),
        ),
        check_vma=False,
    )
```

```python
import functools

import jax
import jax.numpy as jnp
import numpy as np
from jax import lax
from jax.experimental import pallas as pl
from jax.experimental.pallas import tpu as pltpu
from jax.sharding import PartitionSpec as P

HEAD = 128
R = 16
BLK = 128
SEQ = 4096
ROPE_BASE = 500000.0
ADAPTER_SCALE = 2.0
ALL = ("groups", "node", "outer")
HBM = pl.BlockSpec(memory_space=pltpu.HBM)
ANY = pl.BlockSpec(memory_space=pl.ANY)
MIB = 1024 * 1024


def rope_constants():
    half = HEAD // 2
    frequency = ROPE_BASE ** (-2.0 * np.arange(half) / HEAD)
    inside = np.arange(BLK)[:, None] * frequency[None, :]
    starts = BLK * np.arange(SEQ // BLK)[:, None] * frequency[None, :]
    both = lambda t: np.concatenate((t, t), axis=1)
    return np.concatenate(
        (both(np.cos(inside)), both(np.sin(inside)), both(np.cos(starts)), both(np.sin(starts)))
    ).astype(np.float32)


def block_tables(tab_ref, c_row, s_row):
    c_in = tab_ref[0:BLK, :]
    s_in = tab_ref[BLK : 2 * BLK, :]
    cosine = c_in * c_row - s_in * s_row
    sine = s_in * c_row + c_in * s_row
    lane = lax.broadcasted_iota(jnp.int32, (1, HEAD), 1)
    return cosine, jnp.where(lane < HEAD // 2, -sine, sine)


def gradient_kernel(
    sc, tids, count, pos, tok_ref, a_ref, b_ref, cot_ref, tab_ref, low_ref, own_ref, sib_ref,
    tv, av, bv, cv, tab, cosines, sines, grad, low, back, piece, sems,
):
    slots, rows, chunk = tv.shape
    down_half, up_half = chunk // 2, HEAD // 2
    outer = sc[8]
    lane = lax.broadcasted_iota(jnp.int32, (1, HEAD), 1)

    def chunk_copies(i):
        columns = pl.ds(pl.multiple_of(sc[i] * chunk, chunk), chunk)
        heads = pl.ds(pl.multiple_of(i * HEAD, HEAD), HEAD)
        return (
            pltpu.make_async_copy(cot_ref.at[:, heads], cv.at[i], sems.at[0, i]),
            pltpu.make_async_copy(a_ref.at[columns, :], av.at[i], sems.at[1, i]),
            pltpu.make_async_copy(tok_ref.at[:, columns], tv.at[i], sems.at[2, i]),
        )

    small = (
        pltpu.make_async_copy(tab_ref, tab, sems.at[3, 0]), pltpu.make_async_copy(b_ref, bv, sems.at[3, 1]),
    )
    for c in small:
        c.start()
    for i in range(slots):
        for c in chunk_copies(i):
            c.start()
    for c in small:
        c.wait()

    def keep_tables(at, cosine, sine):
        cosines[at, :] = cosine
        sines[at, :] = sine

    rope_blocks(pos, count, tab, rows, keep_tables)
    low[...] = jnp.zeros_like(low)
    back[...] = jnp.zeros_like(back)

    @pl.loop(0, slots)
    def _(i):
        for c in chunk_copies(i):
            c.wait()
        low[...] += jnp.dot(tv[i], av[i], preferred_element_type=jnp.float32)
        x = cv[i].astype(jnp.float32)
        g = (x * cosines[...] - pltpu.roll(x, HEAD // 2, 1) * sines[...]).astype(jnp.bfloat16)
        grad[i] = g
        second = bv[pl.ds(pl.multiple_of(i * HEAD, HEAD), HEAD), :]
        back[...] += jnp.dot(g, second, preferred_element_type=jnp.float32)

    for b in range(rows // BLK):
        at = slice(b * BLK, (b + 1) * BLK)
        hit = jnp.logical_and(lane // R == tids[b], b < count[0])
        select = jnp.where(hit, 1.0, 0.0).astype(jnp.float32)
        low_ref[at, :] = (low[at, :] * select).astype(jnp.bfloat16)
        back[at, :] = ADAPTER_SCALE * (back[at, :] * select).astype(jnp.bfloat16).astype(jnp.float32)
    turned = back[...].astype(jnp.bfloat16)
    contract = (((0,), (0,)), ((), ()))

    @pl.loop(0, slots)
    def _(i):
        for core, out in ((outer, own_ref), (1 - outer, sib_ref)):
            columns = pl.ds(pl.multiple_of(core * down_half, down_half), down_half)
            down = lax.dot_general(turned, tv[i, :, columns], contract, preferred_element_type=jnp.float32)
            out[i, 0:down_half, :] = down.T.astype(out.dtype)
        piece[...] = ADAPTER_SCALE * lax.dot_general(
            grad[sc[i]], low_ref[...], contract, preferred_element_type=jnp.float32
        )
        for core, out in ((outer, own_ref), (1 - outer, sib_ref)):
            at = pl.multiple_of(core * up_half, up_half)
            out[i, down_half:, :] = piece[pl.ds(at, up_half), :].astype(out.dtype)


def product_kernel(held_from, crossed_from, first, joined, sc, *refs):
    refs = list(refs)
    take = lambda n: [refs.pop(0) for _ in range(n)]
    toks = take(2)
    weights = (take(len(held_from)), take(len(crossed_from)))
    given = None if first else (take(2), take(2))
    low_ref, second_ref = take(2) if first else (None, None)
    outs = (take(2), take(1 if joined else 2))
    spare = take(1) if first else []
    tvs, wvs, tots = (take(2) for _ in range(3))
    sems, out_sems = refs
    deep, half = weights[0][-1].shape
    outer, plane = sc[8], sc[9]
    made, saved = [], []
    first_column = lambda side: pl.multiple_of((1 - plane if side else plane) * half, half)

    def load(src, dst):
        c = pltpu.make_async_copy(src, dst, sems.at[len(made)])
        c.start()
        made.append(c)
        return c

    columns = lambda i: pl.ds(pl.multiple_of((2 * sc[i] + outer) * deep, deep), deep)
    need = {}
    for k in range(2):
        for side, sources in enumerate((held_from, crossed_from)):
            todo = need[k, side] = []
            for i, at in enumerate(sources):
                part = slice(i * deep, (i + 1) * deep)
                if k == 0:
                    w = weights[side][i]
                    if w.shape[1] != half:
                        w = w.at[:, pl.ds(first_column(side), half)]
                    todo.append(load(w, wvs[side].at[part, :]))
                todo.append(load(toks[k].at[:, columns(at)], tvs[side].at[k, :, part]))
            if not first:
                todo.append(load(given[k][side], tots[side].at[k]))

    def start(k, side):
        if not first:
            return tots[side][k]
        if k:
            return 0.0
        return ADAPTER_SCALE * lax.dot_general(
            low_ref[...], second_ref[pl.ds(first_column(side), half), :], (((1,), (1,)), ((), ())),
            preferred_element_type=jnp.float32,
        )

    for k in range(2):
        for side in range(2):
            for c in need[k, side]:
                c.wait()
            if first and k == 0 and side:
                c = pltpu.make_async_copy(wvs[1].at[0:deep, :], spare[0], out_sems.at[4])
                c.start()
                saved.append(c)
            tots[side][k] = start(k, side) + jnp.dot(
                tvs[side][k], wvs[side][...], preferred_element_type=jnp.float32
            )
            if k and joined:
                dst = outs[1][0].at[:, side * half : (side + 1) * half]
            else:
                dst = outs[k][side]
            c = pltpu.make_async_copy(tots[side].at[k], dst, out_sems.at[2 * k + side])
            c.start()
            saved.append(c)
    for c in saved:
        c.wait()


def rope_blocks(pos, count, tab_ref, tokens, write):
    starts = SEQ // BLK
    for b in range(tokens // BLK):
        at = pos[b * BLK] // BLK
        cosine, sine = block_tables(
            tab_ref, tab_ref[pl.ds(2 * BLK + at, 1), :], tab_ref[pl.ds(2 * BLK + starts + at, 1), :]
        )
        live = jnp.where(b < count[0], 1.0, 0.0).astype(jnp.float32)
        write(slice(b * BLK, (b + 1) * BLK), cosine * live, sine * live)


def rotate_heads(pre, cosine, sine, res, rows):
    for h in range(pre.shape[1] // HEAD):
        cols = slice(h * HEAD, (h + 1) * HEAD)
        x = pre[:, cols]
        res[rows, cols] = (x * cosine + pltpu.roll(x, HEAD // 2, 1) * sine).astype(jnp.bfloat16)


def load_tokens(sc, tok_ref, nodes, pieces, tv, wv, sems):
    deep = pieces[0].shape[0]
    outer, copies = sc[8], []
    for core in range(2):
        for i, node in enumerate(nodes):
            at = pl.multiple_of((2 * sc[node] + (1 - outer if core else outer)) * deep, deep)
            to = (core * len(nodes) + i) * deep
            copies.append((tok_ref.at[:, pl.ds(at, deep)], tv.at[:, to : to + deep]))
            if not core:
                copies.append((pieces[i], wv.at[i * deep : (i + 1) * deep, :]))
    made = [pltpu.make_async_copy(src, dst, sems.at[i]) for i, (src, dst) in enumerate(copies)]
    for c in made:
        c.start()
    return made


def dots(tok, columns, weights):
    total = None
    for at, w in zip(columns, weights):
        part = jnp.dot(tok[:, at : at + w.shape[0]], w[...], preferred_element_type=jnp.float32)
        total = part if total is None else total + part
    return total


def held_keys_kernel(
    sc, count, pos, tok_ref, mine_h, mine_c, y3, a3, given, y3_other, a3_other, tab_ref,
    keys_ref, total_ref, tv, wv, vh, vc, res, sems,
):
    deep, half = y3.shape
    made = load_tokens(sc, tok_ref, (17, 13), (y3, a3), tv, wv, sems)
    made += [pltpu.make_async_copy(mine_h, vh, sems.at[6]), pltpu.make_async_copy(mine_c, vc, sems.at[7])]
    for c in made[6:]:
        c.start()
    for c in made:
        c.wait()
    vc[...] = (vc[...] + given[:, half:]) + dots(tv, (deep, 3 * deep), (wv.at[deep : 2 * deep, :], a3_other))
    last = pltpu.make_async_copy(vc, total_ref, sems.at[8])
    last.start()

    def write(at, cosine, sine):
        pre = dots(tv.at[at, :], (0, 2 * deep), (wv.at[0:deep, :], y3_other))
        rotate_heads(pre + (vh[at, :] + given[at, 0:half]), cosine, sine, res, at)

    rope_blocks(pos, count, tab_ref, vh.shape[0], write)
    save = pltpu.make_async_copy(
        res, keys_ref.at[:, pl.ds(pl.multiple_of(sc[9] * half, half), half)], sems.at[9]
    )
    save.start()
    save.wait()
    last.wait()


def crossed_kernel(
    sc, tok_ref, sib_ref, total_ref, e1, e2, mine_ref, theirs_ref, last_ref, last_sib_ref, tv, wv, vc, sems, out_sems,
):
    deep = e1.shape[0]
    outer, copies = sc[8], []
    columns = lambda node: pl.ds(pl.multiple_of((2 * sc[node] + outer) * deep, deep), deep)
    for i, (node, piece) in enumerate(((15, e1), (16, e2))):
        part = slice(i * deep, (i + 1) * deep)
        copies.append((piece, wv.at[part, :]))
        for k, tok in enumerate((tok_ref, sib_ref)):
            copies.append((tok.at[:, columns(node)], tv.at[k, :, part]))
    copies.append((total_ref, vc.at[0]))
    for i, node in enumerate((17, 14)):
        copies.append((tok_ref.at[:, columns(node)], last_ref.at[i]))
        copies.append((sib_ref.at[:, columns(node)], last_sib_ref.at[i]))
    made = [pltpu.make_async_copy(src, dst, sems.at[i]) for i, (src, dst) in enumerate(copies)]
    for c in made:
        c.start()
    for c in made[:7]:
        c.wait()
    saves = []
    for k, dst in enumerate((mine_ref, theirs_ref)):
        part = jnp.dot(tv[k], wv[...], preferred_element_type=jnp.float32)
        vc[k] = part if k else vc[0] + part
        saves.append(pltpu.make_async_copy(vc.at[k], dst, out_sems.at[k]))
        saves[-1].start()
    for c in made[7:] + saves:
        c.wait()


def last_kernel(total_ref, tok_ref, e3, e0, out_ref):
    total = total_ref[...]
    for i, w in enumerate((e3, e0)):
        total = total + jnp.dot(tok_ref[i], w[...], preferred_element_type=jnp.float32)
    out_ref[...] = total.astype(out_ref.dtype)


def fold_kernel(keep_ref, got_ref, next_ref, *send_refs):
    at = next_ref.shape[0]
    next_ref[...] = keep_ref[0:at] + got_ref[0:at].astype(jnp.float32)
    for ref in send_refs:
        n = ref.shape[0]
        ref[...] = (keep_ref[at : at + n] + got_ref[at : at + n].astype(jnp.float32)).astype(ref.dtype)
        at += n


def sum_kernel(keep_ref, *refs):
    total = keep_ref[...]
    for ref in refs[:-1]:
        total = total + ref[...].astype(jnp.float32)
    refs[-1][...] = total


def crossed_keys_kernel(
    sc, count, pos, total_ref, given, share, share_other, tab_ref, keys_ref, out_ref, down_ref, up_ref, res, sems,
):
    half = total_ref.shape[1]
    outer = sc[8]
    down_rows = down_ref.shape[0] // 2
    up_rows = up_ref.shape[0] // 2
    saves = []

    def save(src, dst):
        c = pltpu.make_async_copy(src, dst, sems.at[len(saves)])
        c.start()
        saves.append(c)

    for core, sums in ((outer, share), (1 - outer, share_other)):
        down_at = pl.multiple_of(core * down_rows, down_rows)
        up_at = pl.multiple_of(core * up_rows, up_rows)
        save(sums.at[0, 0:down_rows, :], down_ref.at[pl.ds(down_at, down_rows), :])
        save(sums.at[0, down_rows:, :], up_ref.at[pl.ds(up_at, up_rows), :])
    columns = pl.ds(pl.multiple_of((1 - sc[9]) * half, half), half)

    def write(at, cosine, sine):
        rotate_heads(total_ref[at, :] + given[at, :].astype(jnp.float32), cosine, sine, res, at)
        save(res.at[at, :], out_ref.at[at, columns])

    rope_blocks(pos, count, tab_ref, res.shape[0], write)
    for c in saves:
        c.wait()


class Routes:
    def __init__(self, mesh):
        self.groups, self.nodes, self.outers = (mesh.shape[a] for a in ALL)
        self.z = self.nodes // 2
        line = list(range(self.z))
        ring = line[:1] + line[1::2] + line[2::2][::-1]
        self.next = {ring[i]: ring[(i + 1) % self.z] for i in range(self.z)}
        self.prev = {v: k for k, v in self.next.items()}

    def pairs(self, f):
        at = lambda g, z, y, o: (g * self.nodes + 2 * z + y) * self.outers + o
        return [
            (at(g, z, y, o), at(*f(g, z, y, o)))
            for g in range(self.groups)
            for z in range(self.z)
            for y in range(2)
            for o in range(self.outers)
        ]

    def table(self):
        rows = []
        for _, n, o, g in [
            (0, n, o, g) for g in range(self.groups) for n in range(self.nodes) for o in range(self.outers)
        ]:
            z, y = divmod(n, 2)
            slot = [n ^ ((r >> 2) & 1 | ((r >> 1) & 1) << 1 | (r & 1) << 2) for r in range(8)]
            from_z = [z]
            for _ in range(self.z - 1):
                from_z.append(self.prev[from_z[-1]])
            rows.append(
                slot + [o, g] + [2 * k + y for k in from_z] + [2 * k + 1 - y for k in from_z]
            )
        return np.array(rows, np.int32)


def call(kernel, name, shapes, in_specs, out_specs, scratch, args, grid=(), prefetch=1, aliases=None, vmem=16):
    specs = [None] * prefetch + in_specs
    return pl.pallas_call(
        kernel,
        out_shape=shapes,
        grid_spec=pltpu.PrefetchScalarGridSpec(
            num_scalar_prefetch=prefetch, grid=grid, in_specs=in_specs, out_specs=out_specs,
            scratch_shapes=scratch,
        ),
        compiler_params=pltpu.CompilerParams(vmem_limit_bytes=vmem * MIB),
        cost_estimate=pl.CostEstimate(flops=1000, bytes_accessed=1024, transcendentals=0),
        input_output_aliases=aliases or {},
        name=name,
    )(*[pltpu.with_memory_space_constraint(x, pltpu.HBM) if spec is HBM else x for x, spec in zip(args, specs)])


def fast_body(
    routes, tokens, frozen_weight, down_adapter, second_adapter_weight, tenant_ids, block_counts, positions, cotangent
):
    bf16, f32 = jnp.bfloat16, jnp.float32
    rows, width = tokens.shape
    deep, kv = frozen_weight.shape
    nodes = routes.nodes
    chunk = 2 * deep
    half = kv // 2
    rank = down_adapter.shape[1]
    plane = lax.axis_index("groups")
    outer = lax.axis_index("outer")
    tab = jnp.asarray(rope_constants())

    send = lambda x, f: lax.ppermute(x, ALL, routes.pairs(f))
    to_core = lambda g, z, y, o: (g, z, y, 1 - o)
    to_x = lambda g, z, y, o: (1 - g, z, y, o)
    to_y = lambda g, z, y, o: (g, z, 1 - y, o)
    to_z = lambda g, z, y, o: (g, routes.next[z], y, o)
    to_z1 = lambda g, z, y, o: (g, z ^ 1, y, o)
    to_z2 = lambda g, z, y, o: (g, z ^ 2, y, o)
    to_z3 = lambda g, z, y, o: (g, z ^ 3, y, o)
    fence = lambda *x: lax.optimization_barrier(x)
    vm = pl.BlockSpec(memory_space=pltpu.VMEM)
    dma = pltpu.SemaphoreType.DMA
    shape = jax.ShapeDtypeStruct

    def fold(keep, got, stay, *go):
        slots = lambda n, dtype: pltpu.VMEM((n, *keep.shape[1:]), dtype)
        return call(
            fold_kernel, "fold", [slots(stay, f32), *[slots(n, bf16) for n in go]],
            [vm, vm], [vm] * (1 + len(go)), [], (keep, got), prefetch=0,
        )

    def product(held, crossed, given=(), adapters=(), joined=False):
        kh, kc = len(held) * deep, len(crossed) * deep
        outs = [pltpu.VMEM((rows, half), f32)] * 2
        outs += [pltpu.VMEM((rows, kv), f32)] if joined else outs
        outs += [] if given else [shape((deep, half), bf16)]
        return call(
            functools.partial(
                product_kernel, [i for _, i in held], [i for _, i in crossed], not given, joined
            ),
            "products", outs,
            [HBM] * 2 + [HBM if w is frozen_weight else ANY for w, _ in held + crossed] + [ANY] * len(given)
            + [vm] * len(adapters), [ANY] * len(outs),
            [
                pltpu.VMEM((2, rows, kh), bf16), pltpu.VMEM((2, rows, kc), bf16),
                pltpu.VMEM((kh, half), bf16), pltpu.VMEM((kc, half), bf16),
                pltpu.VMEM((2, rows, half), f32), pltpu.VMEM((2, rows, half), f32),
                dma((3 * len(held) + 3 * len(crossed) + 4,)), dma((5,)),
            ],
            (sc, tokens, sib_tokens, *[w for w, _ in held], *[w for w, _ in crossed], *given, *adapters),
        )

    z0 = lax.dynamic_slice(frozen_weight, (0, plane * half), (deep, half))
    z0, own_tokens, table = fence(z0, tokens, jnp.asarray(routes.table()))
    sc = lax.dynamic_slice(table, (lax.axis_index(ALL), 0), (1, table.shape[1]))[0]
    z1 = send(z0, to_z)
    y0 = send(z0, to_y)
    sib_tokens = send(own_tokens, to_core)
    slot_rows = chunk // 2 + kv // nodes // 2
    low, own, sib = call(
        gradient_kernel, "adapter_gradients",
        [
            pltpu.VMEM((rows, rank), bf16), pltpu.VMEM((nodes, slot_rows, rank), f32),
            pltpu.VMEM((nodes, slot_rows, rank), bf16),
        ],
        [HBM] * 5, [vm] * 3,
        [
            pltpu.VMEM((nodes, rows, chunk), bf16), pltpu.VMEM((nodes, chunk, rank), bf16),
            pltpu.VMEM((kv, rank), bf16), pltpu.VMEM((nodes, rows, HEAD), bf16), pltpu.VMEM(tab.shape, f32),
            pltpu.VMEM((rows, HEAD), f32), pltpu.VMEM((rows, HEAD), f32), pltpu.VMEM((nodes, rows, HEAD), bf16),
            pltpu.VMEM((rows, rank), f32), pltpu.VMEM((rows, rank), f32), pltpu.VMEM((HEAD, rank), f32),
            dma((4, nodes)),
        ],
        (sc, tenant_ids, block_counts, positions, tokens, down_adapter, second_adapter_weight, cotangent, tab),
        prefetch=4, vmem=52,
    )
    z1, y0, low, own, sib, sib_tokens = fence(z1, y0, low, own, sib, sib_tokens)

    z2 = send(z1, to_z)
    y1 = send(z1, to_y)
    a1 = send(z1, to_x)
    other = send(sib, to_core)
    *totals, c0 = product(
        ((frozen_weight, 10), (y0, 14), (z1, 11)), ((frozen_weight, 10),), adapters=(low, second_adapter_weight)
    )
    z2, y1, a1, other, *totals = fence(z2, y1, a1, other, *totals)

    z3 = send(z2, to_z)
    y2 = send(z2, to_y)
    a2 = send(z2, to_x)
    keep, out = fold(own, other, 4, 4)
    totals = product(((y1, 15), (z2, 12)), ((a1, 11),), given=totals)
    z3, y2, a2, keep, out, *totals = fence(z3, y2, a2, keep, out, *totals)

    y3 = send(y2, to_z)
    a3 = send(z3, to_x)
    got = send(out, to_y)
    mine_h, mine_c, theirs = product(((y2, 16), (z3, 13)), ((a2, 12),), given=totals, joined=True)
    y3, a3, got, mine_h, mine_c, theirs = fence(y3, a3, got, mine_h, mine_c, theirs)

    given, y3_other, a3_other = send(theirs, to_core), send(y3, to_core), send(a3, to_core)
    e1 = send(y1, to_x)
    e2 = send(a2, to_y)
    keep, *out = fold(keep, got, 1, 1, 1, 1)
    got = [send(x, f) for x, f in zip(out, (to_z2, to_z1, to_z3))]
    own_space = [
        pltpu.VMEM((rows, 2 * chunk), bf16), pltpu.VMEM((chunk, half), bf16), pltpu.VMEM((rows, half), f32),
    ]
    keys, total = call(
        held_keys_kernel, "held_keys", [shape((rows, kv), bf16), pltpu.VMEM((rows, half), f32)],
        [HBM] + [ANY] * 4 + [vm] * 4, [ANY, ANY],
        own_space + [pltpu.VMEM((rows, half), f32), pltpu.VMEM((rows, half), bf16), dma((10,))],
        (sc, block_counts, positions, tokens, mine_h, mine_c, y3, a3, given, y3_other, a3_other, tab),
        prefetch=3,
    )
    y3, c0, total = fence(y3, c0, total)
    e3 = send(y3, to_x)
    e0 = send(c0, to_y)
    e1, e2, total = fence(e1, e2, total)
    *sums, last, last_sib = call(
        crossed_kernel, "crossed_products",
        [pltpu.VMEM((rows, half), f32)] * 2 + [pltpu.VMEM((2, rows, deep), bf16)] * 2,
        [HBM] * 2 + [ANY] * 3, [ANY] * 4,
        [
            pltpu.VMEM((2, rows, chunk), bf16), pltpu.VMEM((chunk, half), bf16),
            pltpu.VMEM((2, rows, half), f32), dma((11,)), dma((2,)),
        ],
        (sc, tokens, sib_tokens, total, e1, e2),
    )
    e3, e0, mine, theirs, last, last_sib, *got = fence(e3, e0, *sums, last, last_sib, *got)

    share = call(
        sum_kernel, "share", pltpu.VMEM(keep.shape, f32), [vm] * 4, vm, [], (keep, *got), prefetch=0,
    )
    finish = lambda total, toks, dtype: call(
        last_kernel, "last_product", pltpu.VMEM((rows, half), dtype), [vm] * 4, vm, [], (total, toks, e3, e0), prefetch=0,
    )
    given = send(finish(theirs, last_sib, bf16), to_core)
    keys, down, up = call(
        crossed_keys_kernel, "crossed_keys",
        [shape((rows, kv), bf16), shape((chunk, rank), f32), shape((kv // nodes, rank), f32)],
        [vm] * 5 + [ANY], [ANY] * 3,
        [pltpu.VMEM((rows, half), bf16), dma((4 + rows // BLK,))],
        (
            sc, block_counts, positions, finish(mine, last, f32), given, share, send(share, to_core), tab, keys,
        ),
        prefetch=3, aliases={8: 0},
    )
    return keys, down, up


def rope_tables(positions):
    half_head = HEAD // 2
    frequency = ROPE_BASE ** (-2.0 * jnp.arange(half_head, dtype=jnp.float32) / HEAD)
    angle = positions.astype(jnp.float32)[:, None] * frequency[None, :]
    return (jnp.cos(angle), jnp.sin(angle))


def rotate(field, cosine, sine, orient):
    rows = field.shape[0]
    shaped = field.reshape(rows, -1, 2, HEAD // 2)
    first = shaped[:, :, 0]
    second = shaped[:, :, 1]
    cos_b = cosine[:, None, :]
    sin_b = orient * sine[:, None, :]
    out_first = first * cos_b - second * sin_b
    out_second = second * cos_b + first * sin_b
    return jnp.stack((out_first, out_second), axis=2).reshape(rows, -1)


def plain_body(
    tokens, frozen_weight, down_adapter, second_adapter_weight, tenant_ids, block_counts, positions, cotangent
):
    token_rows = tokens.shape[0]
    block_total = tenant_ids.shape[0]
    block_rows = token_rows // block_total
    width_cols = down_adapter.shape[1]
    live_blocks = (jnp.arange(block_total, dtype=jnp.int32) < block_counts[0]).astype(jnp.float32)
    live_rows = jnp.repeat(live_blocks, block_rows)[:, None]
    column_tenant = jnp.arange(width_cols, dtype=jnp.int32) // R
    select_blocks = (tenant_ids[:, None] == column_tenant[None, :]).astype(
        jnp.float32
    ) * live_blocks[:, None]
    select = jnp.repeat(select_blocks, block_rows, axis=0)
    lowrank_hidden = (
        jnp.dot(tokens, down_adapter, preferred_element_type=jnp.float32) * select
    ).astype(jnp.bfloat16)
    frozen_output = jnp.dot(
        tokens,
        lax.all_gather(frozen_weight, ("node", "outer"), axis=0, tiled=True),
        preferred_element_type=jnp.float32,
    )
    adapter_output = lax.dot_general(
        lowrank_hidden,
        second_adapter_weight,
        (((1,), (1,)), ((), ())),
        preferred_element_type=jnp.float32,
    )
    unrotated_keys = frozen_output + ADAPTER_SCALE * adapter_output
    cosine, sine = rope_tables(positions)
    keys = (live_rows * rotate(unrotated_keys, cosine, sine, 1.0)).astype(jnp.bfloat16)
    output_gradient = (
        live_rows * rotate(cotangent.astype(jnp.float32), cosine, sine, -1.0)
    ).astype(jnp.bfloat16)
    backward_gradient = (
        jnp.dot(output_gradient, second_adapter_weight, preferred_element_type=jnp.float32) * select
    ).astype(jnp.bfloat16)
    down_product = ADAPTER_SCALE * lax.dot_general(
        tokens, backward_gradient, (((0,), (0,)), ((), ())), preferred_element_type=jnp.float32
    )
    up_product = ADAPTER_SCALE * lax.dot_general(
        output_gradient,
        lowrank_hidden,
        (((0,), (0,)), ((), ())),
        preferred_element_type=jnp.float32,
    )
    shares = (
        lax.psum_scatter(down_product, "node", scatter_dimension=0, tiled=True),
        lax.psum_scatter(up_product, "node", scatter_dimension=0, tiled=True),
    )
    down_adapter_gradient, up_adapter_gradient = lax.psum((shares[0], shares[1]), "outer")
    return (keys, down_adapter_gradient, up_adapter_gradient)


def solution(mesh):
    placed = (
        P(("groups", "node", "outer"), None),
        P(("node", "outer"), None),
        P(),
        P(),
        P(("groups", "node", "outer")),
        P(("groups", "node", "outer")),
        P(("groups", "node", "outer")),
        P(("groups", "node", "outer"), None),
    )
    routed = tuple(mesh.shape[a] for a in ALL) == (2, 8, 2)
    return jax.shard_map(
        functools.partial(fast_body, Routes(mesh)) if routed else plain_body,
        mesh=mesh,
        in_specs=placed,
        out_specs=(
            P(("groups", "node", "outer"), None),
            P(("groups", "node"), None),
            P(("groups", "node"), None),
        ),
        check_vma=False,
    )
```

```python
import functools

import jax
import jax.numpy as jnp
import numpy as np
from jax import lax
from jax.experimental import pallas as pl
from jax.experimental.pallas import tpu as pltpu
from jax.sharding import PartitionSpec as P

HEAD = 128
R = 16
BLK = 128
SEQ = 4096
ROPE_BASE = 500000.0
ADAPTER_SCALE = 2.0
ALL = ("groups", "node", "outer")
HBM = pl.BlockSpec(memory_space=pltpu.HBM)
ANY = pl.BlockSpec(memory_space=pl.ANY)
MIB = 1024 * 1024


def rope_constants():
    half = HEAD // 2
    frequency = ROPE_BASE ** (-2.0 * np.arange(half) / HEAD)
    inside = np.arange(BLK)[:, None] * frequency[None, :]
    starts = BLK * np.arange(SEQ // BLK)[:, None] * frequency[None, :]
    both = lambda t: np.concatenate((t, t), axis=1)
    return np.concatenate(
        (both(np.cos(inside)), both(np.sin(inside)), both(np.cos(starts)), both(np.sin(starts)))
    ).astype(np.float32)


def block_tables(tab_ref, c_row, s_row):
    c_in = tab_ref[0:BLK, :]
    s_in = tab_ref[BLK : 2 * BLK, :]
    cosine = c_in * c_row - s_in * s_row
    sine = s_in * c_row + c_in * s_row
    lane = lax.broadcasted_iota(jnp.int32, (1, HEAD), 1)
    return cosine, jnp.where(lane < HEAD // 2, -sine, sine)


def gradient_kernel(
    sc, tids, count, pos, tok_ref, a_ref, b_ref, cot_ref, tab_ref, low_ref, own_ref, sib_ref,
    tv, av, bv, cv, tab, cosines, sines, grad, low, back, piece, sems,
):
    slots, rows, chunk = tv.shape
    down_half, up_half = chunk // 2, HEAD // 2
    outer = sc[8]
    lane = lax.broadcasted_iota(jnp.int32, (1, HEAD), 1)

    def chunk_copies(i):
        columns = pl.ds(pl.multiple_of(sc[i] * chunk, chunk), chunk)
        heads = pl.ds(pl.multiple_of(i * HEAD, HEAD), HEAD)
        return (
            pltpu.make_async_copy(cot_ref.at[:, heads], cv.at[i], sems.at[0, i]),
            pltpu.make_async_copy(a_ref.at[columns, :], av.at[i], sems.at[1, i]),
            pltpu.make_async_copy(tok_ref.at[:, columns], tv.at[i], sems.at[2, i]),
        )

    small = (
        pltpu.make_async_copy(tab_ref, tab, sems.at[3, 0]), pltpu.make_async_copy(b_ref, bv, sems.at[3, 1]),
    )
    for c in small:
        c.start()
    for i in range(slots):
        for c in chunk_copies(i):
            c.start()
    for c in small:
        c.wait()

    def keep_tables(at, cosine, sine):
        cosines[at, :] = cosine
        sines[at, :] = sine

    rope_blocks(pos, count, tab, rows, keep_tables)
    low[...] = jnp.zeros_like(low)
    back[...] = jnp.zeros_like(back)

    @pl.loop(0, slots)
    def _(i):
        for c in chunk_copies(i):
            c.wait()
        low[...] += jnp.dot(tv[i], av[i], preferred_element_type=jnp.float32)
        x = cv[i].astype(jnp.float32)
        g = (x * cosines[...] - pltpu.roll(x, HEAD // 2, 1) * sines[...]).astype(jnp.bfloat16)
        grad[i] = g
        second = bv[pl.ds(pl.multiple_of(i * HEAD, HEAD), HEAD), :]
        back[...] += jnp.dot(g, second, preferred_element_type=jnp.float32)

    for b in range(rows // BLK):
        at = slice(b * BLK, (b + 1) * BLK)
        hit = jnp.logical_and(lane // R == tids[b], b < count[0])
        select = jnp.where(hit, 1.0, 0.0).astype(jnp.float32)
        low_ref[at, :] = (low[at, :] * select).astype(jnp.bfloat16)
        back[at, :] = ADAPTER_SCALE * (back[at, :] * select).astype(jnp.bfloat16).astype(jnp.float32)
    turned = back[...].astype(jnp.bfloat16)
    contract = (((0,), (0,)), ((), ()))

    @pl.loop(0, slots)
    def _(i):
        for core, out in ((outer, own_ref), (1 - outer, sib_ref)):
            columns = pl.ds(pl.multiple_of(core * down_half, down_half), down_half)
            down = lax.dot_general(turned, tv[i, :, columns], contract, preferred_element_type=jnp.float32)
            out[i, 0:down_half, :] = down.T.astype(out.dtype)
        piece[...] = ADAPTER_SCALE * lax.dot_general(
            grad[sc[i]], low_ref[...], contract, preferred_element_type=jnp.float32
        )
        for core, out in ((outer, own_ref), (1 - outer, sib_ref)):
            at = pl.multiple_of(core * up_half, up_half)
            out[i, down_half:, :] = piece[pl.ds(at, up_half), :].astype(out.dtype)


def product_kernel(held_from, crossed_from, first, joined, sc, *refs):
    refs = list(refs)
    take = lambda n: [refs.pop(0) for _ in range(n)]
    toks = take(2)
    weights = (take(len(held_from)), take(len(crossed_from)))
    given = None if first else (take(2), take(2))
    low_ref, second_ref = take(2) if first else (None, None)
    sides = 2 if crossed_from else 1
    outs = (take(sides), take(1 if joined else sides))
    tvs, wvs, tots = (take(2) for _ in range(3))
    sems, out_sems = refs
    deep, half = weights[0][-1].shape
    outer, plane = sc[8], sc[9]
    made, saved = [], []
    first_column = lambda side: pl.multiple_of((1 - plane if side else plane) * half, half)

    def load(src, dst):
        c = pltpu.make_async_copy(src, dst, sems.at[len(made)])
        c.start()
        made.append(c)
        return c

    columns = lambda i: pl.ds(pl.multiple_of((2 * sc[i] + outer) * deep, deep), deep)
    need = {}
    for k in range(2):
        for side, sources in enumerate((held_from, crossed_from)):
            todo = need[k, side] = []
            for i, at in enumerate(sources):
                part = slice(i * deep, (i + 1) * deep)
                if k == 0:
                    w = weights[side][i]
                    if w.shape[1] != half:
                        w = w.at[:, pl.ds(first_column(side), half)]
                    todo.append(load(w, wvs[side].at[part, :]))
                todo.append(load(toks[k].at[:, columns(at)], tvs[side].at[k, :, part]))
            if not first:
                todo.append(load(given[k][side], tots[side].at[k]))

    def start(k, side):
        if not first:
            return tots[side][k]
        if k:
            return 0.0
        return ADAPTER_SCALE * lax.dot_general(
            low_ref[...], second_ref[pl.ds(first_column(side), half), :], (((1,), (1,)), ((), ())),
            preferred_element_type=jnp.float32,
        )

    for k in range(2):
        for side in range(sides):
            for c in need[k, side]:
                c.wait()
            tots[side][k] = start(k, side) + jnp.dot(
                tvs[side][k], wvs[side][...], preferred_element_type=jnp.float32
            )
            if k and joined:
                dst = outs[1][0].at[:, side * half : (side + 1) * half]
            else:
                dst = outs[k][side]
            c = pltpu.make_async_copy(tots[side].at[k], dst, out_sems.at[2 * k + side])
            c.start()
            saved.append(c)
    for c in saved:
        c.wait()


def own_crossed_kernel(
    core, passed, sc, tok_ref, sib_ref, w_ref, low_ref, second_ref, *refs
):
    mine_ref, theirs_ref, own_ref, tv, sems = refs[passed:]

    @pl.when(sc[8] == core)
    def _():
        deep, half = own_ref.shape
        at = pl.multiple_of((1 - sc[9]) * half, half)
        columns = pl.ds(pl.multiple_of((2 * sc[10] + sc[8]) * deep, deep), deep)
        loads = [
            pltpu.make_async_copy(w_ref.at[:, pl.ds(at, half)], own_ref, sems.at[0]),
            pltpu.make_async_copy(tok_ref.at[:, columns], tv.at[0], sems.at[1]),
            pltpu.make_async_copy(sib_ref.at[:, columns], tv.at[1], sems.at[2]),
        ]
        for c in loads:
            c.start()
        for c in loads:
            c.wait()
        adapters = ADAPTER_SCALE * lax.dot_general(
            low_ref[...], second_ref[pl.ds(at, half), :], (((1,), (1,)), ((), ())),
            preferred_element_type=jnp.float32,
        )
        mine_ref[...] = adapters + jnp.dot(tv[0], own_ref[...], preferred_element_type=jnp.float32)
        theirs_ref[...] = jnp.dot(tv[1], own_ref[...], preferred_element_type=jnp.float32)


def rope_blocks(pos, count, tab_ref, tokens, write):
    starts = SEQ // BLK
    for b in range(tokens // BLK):
        at = pos[b * BLK] // BLK
        cosine, sine = block_tables(
            tab_ref, tab_ref[pl.ds(2 * BLK + at, 1), :], tab_ref[pl.ds(2 * BLK + starts + at, 1), :]
        )
        live = jnp.where(b < count[0], 1.0, 0.0).astype(jnp.float32)
        write(slice(b * BLK, (b + 1) * BLK), cosine * live, sine * live)


def rotate_heads(pre, cosine, sine, res, rows):
    for h in range(pre.shape[1] // HEAD):
        cols = slice(h * HEAD, (h + 1) * HEAD)
        x = pre[:, cols]
        res[rows, cols] = (x * cosine + pltpu.roll(x, HEAD // 2, 1) * sine).astype(jnp.bfloat16)


def load_tokens(sc, tok_ref, nodes, pieces, tv, wv, sems):
    deep = pieces[0].shape[0]
    outer, copies = sc[8], []
    for core in range(2):
        for i, node in enumerate(nodes):
            at = pl.multiple_of((2 * sc[node] + (1 - outer if core else outer)) * deep, deep)
            to = (core * len(nodes) + i) * deep
            copies.append((tok_ref.at[:, pl.ds(at, deep)], tv.at[:, to : to + deep]))
            if not core:
                copies.append((pieces[i], wv.at[i * deep : (i + 1) * deep, :]))
    made = [pltpu.make_async_copy(src, dst, sems.at[i]) for i, (src, dst) in enumerate(copies)]
    for c in made:
        c.start()
    return made


def dots(tok, columns, weights):
    total = None
    for at, w in zip(columns, weights):
        part = jnp.dot(tok[:, at : at + w.shape[0]], w[...], preferred_element_type=jnp.float32)
        total = part if total is None else total + part
    return total


def held_keys_kernel(
    sc, count, pos, tok_ref, mine_h, mine_c, y3, a3, given, y3_other, a3_other, tab_ref,
    keys_ref, total_ref, tv, wv, vh, vc, res, sems,
):
    deep, half = y3.shape
    made = load_tokens(sc, tok_ref, (17, 13), (y3, a3), tv, wv, sems)
    made += [pltpu.make_async_copy(mine_h, vh, sems.at[6]), pltpu.make_async_copy(mine_c, vc, sems.at[7])]
    for c in made[6:]:
        c.start()
    for c in made:
        c.wait()
    vc[...] = (vc[...] + given[:, half:]) + dots(tv, (deep, 3 * deep), (wv.at[deep : 2 * deep, :], a3_other))
    last = pltpu.make_async_copy(vc, total_ref, sems.at[8])
    last.start()

    def write(at, cosine, sine):
        pre = dots(tv.at[at, :], (0, 2 * deep), (wv.at[0:deep, :], y3_other))
        rotate_heads(pre + (vh[at, :] + given[at, 0:half]), cosine, sine, res, at)

    rope_blocks(pos, count, tab_ref, vh.shape[0], write)
    save = pltpu.make_async_copy(
        res, keys_ref.at[:, pl.ds(pl.multiple_of(sc[9] * half, half), half)], sems.at[9]
    )
    save.start()
    save.wait()
    last.wait()


def crossed_kernel(
    sc, tok_ref, sib_ref, total_ref, e1, e2, mine_ref, theirs_ref, last_ref, last_sib_ref, tv, wv, vc, sems, out_sems,
):
    deep = e1.shape[0]
    outer, copies = sc[8], []
    columns = lambda node: pl.ds(pl.multiple_of((2 * sc[node] + outer) * deep, deep), deep)
    for i, (node, piece) in enumerate(((15, e1), (16, e2))):
        part = slice(i * deep, (i + 1) * deep)
        copies.append((piece, wv.at[part, :]))
        for k, tok in enumerate((tok_ref, sib_ref)):
            copies.append((tok.at[:, columns(node)], tv.at[k, :, part]))
    copies.append((total_ref, vc.at[0]))
    for i, node in enumerate((17, 14)):
        copies.append((tok_ref.at[:, columns(node)], last_ref.at[i]))
        copies.append((sib_ref.at[:, columns(node)], last_sib_ref.at[i]))
    made = [pltpu.make_async_copy(src, dst, sems.at[i]) for i, (src, dst) in enumerate(copies)]
    for c in made:
        c.start()
    for c in made[:7]:
        c.wait()
    saves = []
    for k, dst in enumerate((mine_ref, theirs_ref)):
        part = jnp.dot(tv[k], wv[...], preferred_element_type=jnp.float32)
        vc[k] = part if k else vc[0] + part
        saves.append(pltpu.make_async_copy(vc.at[k], dst, out_sems.at[k]))
        saves[-1].start()
    for c in made[7:] + saves:
        c.wait()


def last_kernel(total_ref, tok_ref, e3, e0, out_ref):
    total = total_ref[...]
    for i, w in enumerate((e3, e0)):
        total = total + jnp.dot(tok_ref[i], w[...], preferred_element_type=jnp.float32)
    out_ref[...] = total.astype(out_ref.dtype)


def fold_kernel(keep_ref, got_ref, next_ref, *send_refs):
    at = next_ref.shape[0]
    next_ref[...] = keep_ref[0:at] + got_ref[0:at].astype(jnp.float32)
    for ref in send_refs:
        n = ref.shape[0]
        ref[...] = (keep_ref[at : at + n] + got_ref[at : at + n].astype(jnp.float32)).astype(ref.dtype)
        at += n


def sum_kernel(keep_ref, *refs):
    total = keep_ref[...]
    for ref in refs[:-1]:
        total = total + ref[...].astype(jnp.float32)
    refs[-1][...] = total


def crossed_keys_kernel(
    sc, count, pos, total_ref, given, share, share_other, tab_ref, keys_ref, out_ref, down_ref, up_ref, res, sems,
):
    half = total_ref.shape[1]
    outer = sc[8]
    down_rows = down_ref.shape[0] // 2
    up_rows = up_ref.shape[0] // 2
    saves = []

    def save(src, dst):
        c = pltpu.make_async_copy(src, dst, sems.at[len(saves)])
        c.start()
        saves.append(c)

    for core, sums in ((outer, share), (1 - outer, share_other)):
        down_at = pl.multiple_of(core * down_rows, down_rows)
        up_at = pl.multiple_of(core * up_rows, up_rows)
        save(sums.at[0, 0:down_rows, :], down_ref.at[pl.ds(down_at, down_rows), :])
        save(sums.at[0, down_rows:, :], up_ref.at[pl.ds(up_at, up_rows), :])
    columns = pl.ds(pl.multiple_of((1 - sc[9]) * half, half), half)

    def write(at, cosine, sine):
        rotate_heads(total_ref[at, :] + given[at, :].astype(jnp.float32), cosine, sine, res, at)
        save(res.at[at, :], out_ref.at[at, columns])

    rope_blocks(pos, count, tab_ref, res.shape[0], write)
    for c in saves:
        c.wait()


class Routes:
    def __init__(self, mesh):
        self.groups, self.nodes, self.outers = (mesh.shape[a] for a in ALL)
        self.z = self.nodes // 2
        line = list(range(self.z))
        ring = line[:1] + line[1::2] + line[2::2][::-1]
        self.next = {ring[i]: ring[(i + 1) % self.z] for i in range(self.z)}
        self.prev = {v: k for k, v in self.next.items()}

    def pairs(self, f):
        at = lambda g, z, y, o: (g * self.nodes + 2 * z + y) * self.outers + o
        return [
            (at(g, z, y, o), at(*f(g, z, y, o)))
            for g in range(self.groups)
            for z in range(self.z)
            for y in range(2)
            for o in range(self.outers)
        ]

    def table(self):
        rows = []
        for _, n, o, g in [
            (0, n, o, g) for g in range(self.groups) for n in range(self.nodes) for o in range(self.outers)
        ]:
            z, y = divmod(n, 2)
            slot = [n ^ ((r >> 2) & 1 | ((r >> 1) & 1) << 1 | (r & 1) << 2) for r in range(8)]
            from_z = [z]
            for _ in range(self.z - 1):
                from_z.append(self.prev[from_z[-1]])
            rows.append(
                slot + [o, g] + [2 * k + y for k in from_z] + [2 * k + 1 - y for k in from_z]
            )
        return np.array(rows, np.int32)


def call(kernel, name, shapes, in_specs, out_specs, scratch, args, grid=(), prefetch=1, aliases=None, vmem=16):
    specs = [None] * prefetch + in_specs
    return pl.pallas_call(
        kernel,
        out_shape=shapes,
        grid_spec=pltpu.PrefetchScalarGridSpec(
            num_scalar_prefetch=prefetch, grid=grid, in_specs=in_specs, out_specs=out_specs,
            scratch_shapes=scratch,
        ),
        compiler_params=pltpu.CompilerParams(vmem_limit_bytes=vmem * MIB),
        cost_estimate=pl.CostEstimate(flops=1000, bytes_accessed=1024, transcendentals=0),
        input_output_aliases=aliases or {},
        name=name,
    )(*[pltpu.with_memory_space_constraint(x, pltpu.HBM) if spec is HBM else x for x, spec in zip(args, specs)])


def fast_body(
    routes, tokens, frozen_weight, down_adapter, second_adapter_weight, tenant_ids, block_counts, positions, cotangent
):
    bf16, f32 = jnp.bfloat16, jnp.float32
    rows, width = tokens.shape
    deep, kv = frozen_weight.shape
    nodes = routes.nodes
    chunk = 2 * deep
    half = kv // 2
    rank = down_adapter.shape[1]
    plane = lax.axis_index("groups")
    outer = lax.axis_index("outer")
    tab = jnp.asarray(rope_constants())

    send = lambda x, f: lax.ppermute(x, ALL, routes.pairs(f))
    to_core = lambda g, z, y, o: (g, z, y, 1 - o)
    to_x = lambda g, z, y, o: (1 - g, z, y, o)
    to_y = lambda g, z, y, o: (g, z, 1 - y, o)
    to_z = lambda g, z, y, o: (g, routes.next[z], y, o)
    to_z1 = lambda g, z, y, o: (g, z ^ 1, y, o)
    to_z2 = lambda g, z, y, o: (g, z ^ 2, y, o)
    to_z3 = lambda g, z, y, o: (g, z ^ 3, y, o)
    fence = lambda *x: lax.optimization_barrier(x)
    vm = pl.BlockSpec(memory_space=pltpu.VMEM)
    dma = pltpu.SemaphoreType.DMA
    shape = jax.ShapeDtypeStruct

    def fold(keep, got, stay, *go):
        slots = lambda n, dtype: pltpu.VMEM((n, *keep.shape[1:]), dtype)
        return call(
            fold_kernel, "fold", [slots(stay, f32), *[slots(n, bf16) for n in go]],
            [vm, vm], [vm] * (1 + len(go)), [], (keep, got), prefetch=0,
        )

    def product(held, crossed, given=(), adapters=(), joined=False):
        kh, kc = len(held) * deep, max(len(crossed), 1) * deep
        outs = [pltpu.VMEM((rows, half), f32)] * (2 if crossed else 1)
        outs += [pltpu.VMEM((rows, kv), f32)] if joined else outs
        return call(
            functools.partial(
                product_kernel, [i for _, i in held], [i for _, i in crossed], not given, joined
            ),
            "products", outs,
            [HBM] * 2 + [HBM if w is frozen_weight else ANY for w, _ in held + crossed] + [ANY] * len(given)
            + [vm] * len(adapters), [ANY] * len(outs),
            [
                pltpu.VMEM((2, rows, kh), bf16), pltpu.VMEM((2, rows, kc), bf16),
                pltpu.VMEM((kh, half), bf16), pltpu.VMEM((kc, half), bf16),
                pltpu.VMEM((2, rows, half), f32), pltpu.VMEM((2, rows, half), f32),
                dma((3 * len(held) + 3 * len(crossed) + 4,)), dma((5,)),
            ],
            (sc, tokens, sib_tokens, *[w for w, _ in held], *[w for w, _ in crossed], *given, *adapters),
        )

    z0 = lax.dynamic_slice(frozen_weight, (0, plane * half), (deep, half))
    z0, own_tokens, table = fence(z0, tokens, jnp.asarray(routes.table()))
    sc = lax.dynamic_slice(table, (lax.axis_index(ALL), 0), (1, table.shape[1]))[0]
    z1 = send(z0, to_z)
    y0 = send(z0, to_y)
    sib_tokens = send(own_tokens, to_core)
    slot_rows = chunk // 2 + kv // nodes // 2
    low, own, sib = call(
        gradient_kernel, "adapter_gradients",
        [
            pltpu.VMEM((rows, rank), bf16), pltpu.VMEM((nodes, slot_rows, rank), f32),
            pltpu.VMEM((nodes, slot_rows, rank), bf16),
        ],
        [HBM] * 5, [vm] * 3,
        [
            pltpu.VMEM((nodes, rows, chunk), bf16), pltpu.VMEM((nodes, chunk, rank), bf16),
            pltpu.VMEM((kv, rank), bf16), pltpu.VMEM((nodes, rows, HEAD), bf16), pltpu.VMEM(tab.shape, f32),
            pltpu.VMEM((rows, HEAD), f32), pltpu.VMEM((rows, HEAD), f32), pltpu.VMEM((nodes, rows, HEAD), bf16),
            pltpu.VMEM((rows, rank), f32), pltpu.VMEM((rows, rank), f32), pltpu.VMEM((HEAD, rank), f32),
            dma((4, nodes)),
        ],
        (sc, tenant_ids, block_counts, positions, tokens, down_adapter, second_adapter_weight, cotangent, tab),
        prefetch=4, vmem=52,
    )
    z1, y0, low, own, sib, sib_tokens = fence(z1, y0, low, own, sib, sib_tokens)

    def own_crossed(core, *given):
        return call(
            functools.partial(own_crossed_kernel, core, len(given)), "own_crossed",
            [pltpu.VMEM((rows, half), f32)] * 2 + [pltpu.VMEM((deep, half), bf16)],
            [HBM] * 3 + [vm] * (2 + len(given)), [vm] * 3, [pltpu.VMEM((2, rows, deep), bf16), dma((3,))],
            (sc, tokens, sib_tokens, frozen_weight, low, second_adapter_weight, *given),
            aliases={6 + i: i for i in range(len(given))},
        )

    other = send(sib, to_core)
    started = own_crossed(0)
    z1, *started = fence(z1, *started)
    z2 = send(z1, to_z)
    y1 = send(z1, to_y)
    a1 = send(z1, to_x)
    crossed_sum, crossed_sib, c0 = own_crossed(1, *started)
    held_sum, held_sib = product(
        ((frozen_weight, 10), (y0, 14), (z1, 11)), (), adapters=(low, second_adapter_weight)
    )
    totals = held_sum, crossed_sum, held_sib, crossed_sib
    z2, y1, a1, other, *totals = fence(z2, y1, a1, other, *totals)

    z3 = send(z2, to_z)
    y2 = send(z2, to_y)
    a2 = send(z2, to_x)
    keep, out = fold(own, other, 4, 4)
    totals = product(((y1, 15), (z2, 12)), ((a1, 11),), given=totals)
    z3, y2, a2, keep, out, *totals = fence(z3, y2, a2, keep, out, *totals)

    y3 = send(y2, to_z)
    a3 = send(z3, to_x)
    got = send(out, to_y)
    mine_h, mine_c, theirs = product(((y2, 16), (z3, 13)), ((a2, 12),), given=totals, joined=True)
    y3, a3, got, mine_h, mine_c, theirs = fence(y3, a3, got, mine_h, mine_c, theirs)

    given, y3_other, a3_other = send(theirs, to_core), send(y3, to_core), send(a3, to_core)
    e1 = send(y1, to_x)
    e2 = send(a2, to_y)
    keep, *out = fold(keep, got, 1, 1, 1, 1)
    got = [send(x, f) for x, f in zip(out, (to_z2, to_z1, to_z3))]
    own_space = [
        pltpu.VMEM((rows, 2 * chunk), bf16), pltpu.VMEM((chunk, half), bf16), pltpu.VMEM((rows, half), f32),
    ]
    keys, total = call(
        held_keys_kernel, "held_keys", [shape((rows, kv), bf16), pltpu.VMEM((rows, half), f32)],
        [HBM] + [ANY] * 4 + [vm] * 4, [ANY, ANY],
        own_space + [pltpu.VMEM((rows, half), f32), pltpu.VMEM((rows, half), bf16), dma((10,))],
        (sc, block_counts, positions, tokens, mine_h, mine_c, y3, a3, given, y3_other, a3_other, tab),
        prefetch=3,
    )
    y3, c0, total = fence(y3, c0, total)
    e3 = send(y3, to_x)
    e0 = send(c0, to_y)
    e1, e2, total = fence(e1, e2, total)
    *sums, last, last_sib = call(
        crossed_kernel, "crossed_products",
        [pltpu.VMEM((rows, half), f32)] * 2 + [pltpu.VMEM((2, rows, deep), bf16)] * 2,
        [HBM] * 2 + [ANY] * 3, [ANY] * 4,
        [
            pltpu.VMEM((2, rows, chunk), bf16), pltpu.VMEM((chunk, half), bf16),
            pltpu.VMEM((2, rows, half), f32), dma((11,)), dma((2,)),
        ],
        (sc, tokens, sib_tokens, total, e1, e2),
    )
    e3, e0, mine, theirs, last, last_sib, *got = fence(e3, e0, *sums, last, last_sib, *got)

    share = call(
        sum_kernel, "share", pltpu.VMEM(keep.shape, f32), [vm] * 4, vm, [], (keep, *got), prefetch=0,
    )
    finish = lambda total, toks, dtype: call(
        last_kernel, "last_product", pltpu.VMEM((rows, half), dtype), [vm] * 4, vm, [], (total, toks, e3, e0), prefetch=0,
    )
    given = send(finish(theirs, last_sib, bf16), to_core)
    keys, down, up = call(
        crossed_keys_kernel, "crossed_keys",
        [shape((rows, kv), bf16), shape((chunk, rank), f32), shape((kv // nodes, rank), f32)],
        [vm] * 5 + [ANY], [ANY] * 3,
        [pltpu.VMEM((rows, half), bf16), dma((4 + rows // BLK,))],
        (
            sc, block_counts, positions, finish(mine, last, f32), given, share, send(share, to_core), tab, keys,
        ),
        prefetch=3, aliases={8: 0},
    )
    return keys, down, up


def rope_tables(positions):
    half_head = HEAD // 2
    frequency = ROPE_BASE ** (-2.0 * jnp.arange(half_head, dtype=jnp.float32) / HEAD)
    angle = positions.astype(jnp.float32)[:, None] * frequency[None, :]
    return (jnp.cos(angle), jnp.sin(angle))


def rotate(field, cosine, sine, orient):
    rows = field.shape[0]
    shaped = field.reshape(rows, -1, 2, HEAD // 2)
    first = shaped[:, :, 0]
    second = shaped[:, :, 1]
    cos_b = cosine[:, None, :]
    sin_b = orient * sine[:, None, :]
    out_first = first * cos_b - second * sin_b
    out_second = second * cos_b + first * sin_b
    return jnp.stack((out_first, out_second), axis=2).reshape(rows, -1)


def plain_body(
    tokens, frozen_weight, down_adapter, second_adapter_weight, tenant_ids, block_counts, positions, cotangent
):
    token_rows = tokens.shape[0]
    block_total = tenant_ids.shape[0]
    block_rows = token_rows // block_total
    width_cols = down_adapter.shape[1]
    live_blocks = (jnp.arange(block_total, dtype=jnp.int32) < block_counts[0]).astype(jnp.float32)
    live_rows = jnp.repeat(live_blocks, block_rows)[:, None]
    column_tenant = jnp.arange(width_cols, dtype=jnp.int32) // R
    select_blocks = (tenant_ids[:, None] == column_tenant[None, :]).astype(
        jnp.float32
    ) * live_blocks[:, None]
    select = jnp.repeat(select_blocks, block_rows, axis=0)
    lowrank_hidden = (
        jnp.dot(tokens, down_adapter, preferred_element_type=jnp.float32) * select
    ).astype(jnp.bfloat16)
    frozen_output = jnp.dot(
        tokens,
        lax.all_gather(frozen_weight, ("node", "outer"), axis=0, tiled=True),
        preferred_element_type=jnp.float32,
    )
    adapter_output = lax.dot_general(
        lowrank_hidden,
        second_adapter_weight,
        (((1,), (1,)), ((), ())),
        preferred_element_type=jnp.float32,
    )
    unrotated_keys = frozen_output + ADAPTER_SCALE * adapter_output
    cosine, sine = rope_tables(positions)
    keys = (live_rows * rotate(unrotated_keys, cosine, sine, 1.0)).astype(jnp.bfloat16)
    output_gradient = (
        live_rows * rotate(cotangent.astype(jnp.float32), cosine, sine, -1.0)
    ).astype(jnp.bfloat16)
    backward_gradient = (
        jnp.dot(output_gradient, second_adapter_weight, preferred_element_type=jnp.float32) * select
    ).astype(jnp.bfloat16)
    down_product = ADAPTER_SCALE * lax.dot_general(
        tokens, backward_gradient, (((0,), (0,)), ((), ())), preferred_element_type=jnp.float32
    )
    up_product = ADAPTER_SCALE * lax.dot_general(
        output_gradient,
        lowrank_hidden,
        (((0,), (0,)), ((), ())),
        preferred_element_type=jnp.float32,
    )
    shares = (
        lax.psum_scatter(down_product, "node", scatter_dimension=0, tiled=True),
        lax.psum_scatter(up_product, "node", scatter_dimension=0, tiled=True),
    )
    down_adapter_gradient, up_adapter_gradient = lax.psum((shares[0], shares[1]), "outer")
    return (keys, down_adapter_gradient, up_adapter_gradient)


def solution(mesh):
    placed = (
        P(("groups", "node", "outer"), None),
        P(("node", "outer"), None),
        P(),
        P(),
        P(("groups", "node", "outer")),
        P(("groups", "node", "outer")),
        P(("groups", "node", "outer")),
        P(("groups", "node", "outer"), None),
    )
    routed = tuple(mesh.shape[a] for a in ALL) == (2, 8, 2)
    return jax.shard_map(
        functools.partial(fast_body, Routes(mesh)) if routed else plain_body,
        mesh=mesh,
        in_specs=placed,
        out_specs=(
            P(("groups", "node", "outer"), None),
            P(("groups", "node"), None),
            P(("groups", "node"), None),
        ),
        check_vma=False,
    )
```

```python
import functools

import jax
import jax.numpy as jnp
import numpy as np
from jax import lax
from jax.experimental import pallas as pl
from jax.experimental.pallas import tpu as pltpu
from jax.sharding import PartitionSpec as P

HEAD = 128
R = 16
BLK = 128
SEQ = 4096
ROPE_BASE = 500000.0
ADAPTER_SCALE = 2.0
ALL = ("groups", "node", "outer")
HBM = pl.BlockSpec(memory_space=pltpu.HBM)
ANY = pl.BlockSpec(memory_space=pl.ANY)
MIB = 1024 * 1024


def rope_constants():
    half = HEAD // 2
    frequency = ROPE_BASE ** (-2.0 * np.arange(half) / HEAD)
    inside = np.arange(BLK)[:, None] * frequency[None, :]
    starts = BLK * np.arange(SEQ // BLK)[:, None] * frequency[None, :]
    both = lambda t: np.concatenate((t, t), axis=1)
    return np.concatenate(
        (both(np.cos(inside)), both(np.sin(inside)), both(np.cos(starts)), both(np.sin(starts)))
    ).astype(np.float32)


def block_tables(tab_ref, c_row, s_row):
    c_in = tab_ref[0:BLK, :]
    s_in = tab_ref[BLK : 2 * BLK, :]
    cosine = c_in * c_row - s_in * s_row
    sine = s_in * c_row + c_in * s_row
    lane = lax.broadcasted_iota(jnp.int32, (1, HEAD), 1)
    return cosine, jnp.where(lane < HEAD // 2, -sine, sine)


def gradient_kernel(
    sc, tids, count, pos, tok_ref, a_ref, b_ref, cot_ref, tab_ref, low_ref, own_ref, sib_ref,
    tv, av, bv, cv, tab, cosines, sines, grad, low, back, piece, sems,
):
    slots, rows, chunk = tv.shape
    down_half, up_half = chunk // 2, HEAD // 2
    outer = sc[8]
    lane = lax.broadcasted_iota(jnp.int32, (1, HEAD), 1)

    def chunk_copies(i):
        columns = pl.ds(pl.multiple_of(sc[i] * chunk, chunk), chunk)
        heads = pl.ds(pl.multiple_of(i * HEAD, HEAD), HEAD)
        return (
            pltpu.make_async_copy(cot_ref.at[:, heads], cv.at[i], sems.at[0, i]),
            pltpu.make_async_copy(a_ref.at[columns, :], av.at[i], sems.at[1, i]),
            pltpu.make_async_copy(tok_ref.at[:, columns], tv.at[i], sems.at[2, i]),
        )

    small = (
        pltpu.make_async_copy(tab_ref, tab, sems.at[3, 0]), pltpu.make_async_copy(b_ref, bv, sems.at[3, 1]),
    )
    for c in small:
        c.start()
    for i in range(slots):
        for c in chunk_copies(i):
            c.start()
    for c in small:
        c.wait()

    def keep_tables(at, cosine, sine):
        cosines[at, :] = cosine
        sines[at, :] = sine

    rope_blocks(pos, count, tab, rows, keep_tables)
    low[...] = jnp.zeros_like(low)
    back[...] = jnp.zeros_like(back)

    @pl.loop(0, slots)
    def _(i):
        for c in chunk_copies(i):
            c.wait()
        low[...] += jnp.dot(tv[i], av[i], preferred_element_type=jnp.float32)
        x = cv[i].astype(jnp.float32)
        g = (x * cosines[...] - pltpu.roll(x, HEAD // 2, 1) * sines[...]).astype(jnp.bfloat16)
        grad[i] = g
        second = bv[pl.ds(pl.multiple_of(i * HEAD, HEAD), HEAD), :]
        back[...] += jnp.dot(g, second, preferred_element_type=jnp.float32)

    for b in range(rows // BLK):
        at = slice(b * BLK, (b + 1) * BLK)
        hit = jnp.logical_and(lane // R == tids[b], b < count[0])
        select = jnp.where(hit, 1.0, 0.0).astype(jnp.float32)
        low_ref[at, :] = (low[at, :] * select).astype(jnp.bfloat16)
        back[at, :] = ADAPTER_SCALE * (back[at, :] * select).astype(jnp.bfloat16).astype(jnp.float32)
    turned = back[...].astype(jnp.bfloat16)
    contract = (((0,), (0,)), ((), ()))

    @pl.loop(0, slots)
    def _(i):
        for core, out in ((outer, own_ref), (1 - outer, sib_ref)):
            columns = pl.ds(pl.multiple_of(core * down_half, down_half), down_half)
            down = lax.dot_general(turned, tv[i, :, columns], contract, preferred_element_type=jnp.float32)
            out[i, 0:down_half, :] = down.T.astype(out.dtype)
        piece[...] = ADAPTER_SCALE * lax.dot_general(
            grad[sc[i]], low_ref[...], contract, preferred_element_type=jnp.float32
        )
        for core, out in ((outer, own_ref), (1 - outer, sib_ref)):
            at = pl.multiple_of(core * up_half, up_half)
            out[i, down_half:, :] = piece[pl.ds(at, up_half), :].astype(out.dtype)


def product_kernel(held_from, crossed_from, first, joined, sc, *refs):
    refs = list(refs)
    take = lambda n: [refs.pop(0) for _ in range(n)]
    toks = take(2)
    weights = (take(len(held_from)), take(len(crossed_from)))
    given = None if first else (take(2), take(2))
    low_ref, second_ref = take(2) if first else (None, None)
    sides = 2 if crossed_from else 1
    outs = (take(sides), take(1 if joined else sides))
    tvs, wvs, tots = (take(2) for _ in range(3))
    sems, out_sems = refs
    deep, half = weights[0][-1].shape
    outer, plane = sc[8], sc[9]
    made, saved = [], []
    first_column = lambda side: pl.multiple_of((1 - plane if side else plane) * half, half)

    def load(src, dst):
        c = pltpu.make_async_copy(src, dst, sems.at[len(made)])
        c.start()
        made.append(c)
        return c

    columns = lambda i: pl.ds(pl.multiple_of((2 * sc[i] + outer) * deep, deep), deep)
    need = {}
    for k in range(2):
        for side, sources in enumerate((held_from, crossed_from)):
            todo = need[k, side] = []
            for i, at in enumerate(sources):
                part = slice(i * deep, (i + 1) * deep)
                if k == 0:
                    w = weights[side][i]
                    if w.shape[1] != half:
                        w = w.at[:, pl.ds(first_column(side), half)]
                    todo.append(load(w, wvs[side].at[part, :]))
                todo.append(load(toks[k].at[:, columns(at)], tvs[side].at[k, :, part]))
            if not first:
                todo.append(load(given[k][side], tots[side].at[k]))

    def start(k, side):
        if not first:
            return tots[side][k]
        if k:
            return 0.0
        return ADAPTER_SCALE * lax.dot_general(
            low_ref[...], second_ref[pl.ds(first_column(side), half), :], (((1,), (1,)), ((), ())),
            preferred_element_type=jnp.float32,
        )

    for k in range(2):
        for side in range(sides):
            for c in need[k, side]:
                c.wait()
            tots[side][k] = start(k, side) + jnp.dot(
                tvs[side][k], wvs[side][...], preferred_element_type=jnp.float32
            )
            if k and joined:
                dst = outs[1][0].at[:, side * half : (side + 1) * half]
            else:
                dst = outs[k][side]
            c = pltpu.make_async_copy(tots[side].at[k], dst, out_sems.at[2 * k + side])
            c.start()
            saved.append(c)
    for c in saved:
        c.wait()


def own_crossed_kernel(
    core, passed, sc, tok_ref, sib_ref, w_ref, low_ref, second_ref, *refs
):
    mine_ref, theirs_ref, own_ref, tv, sems = refs[passed:]

    @pl.when(sc[8] == core)
    def _():
        deep, half = own_ref.shape
        at = pl.multiple_of((1 - sc[9]) * half, half)
        columns = pl.ds(pl.multiple_of((2 * sc[10] + sc[8]) * deep, deep), deep)
        loads = [
            pltpu.make_async_copy(w_ref.at[:, pl.ds(at, half)], own_ref, sems.at[0]),
            pltpu.make_async_copy(tok_ref.at[:, columns], tv.at[0], sems.at[1]),
            pltpu.make_async_copy(sib_ref.at[:, columns], tv.at[1], sems.at[2]),
        ]
        for c in loads:
            c.start()
        for c in loads:
            c.wait()
        adapters = ADAPTER_SCALE * lax.dot_general(
            low_ref[...], second_ref[pl.ds(at, half), :], (((1,), (1,)), ((), ())),
            preferred_element_type=jnp.float32,
        )
        mine_ref[...] = adapters + jnp.dot(tv[0], own_ref[...], preferred_element_type=jnp.float32)
        theirs_ref[...] = jnp.dot(tv[1], own_ref[...], preferred_element_type=jnp.float32)


def rope_blocks(pos, count, tab_ref, tokens, write):
    starts = SEQ // BLK
    for b in range(tokens // BLK):
        at = pos[b * BLK] // BLK
        cosine, sine = block_tables(
            tab_ref, tab_ref[pl.ds(2 * BLK + at, 1), :], tab_ref[pl.ds(2 * BLK + starts + at, 1), :]
        )
        live = jnp.where(b < count[0], 1.0, 0.0).astype(jnp.float32)
        write(slice(b * BLK, (b + 1) * BLK), cosine * live, sine * live)


def rotate_heads(pre, cosine, sine, res, rows):
    for h in range(pre.shape[1] // HEAD):
        cols = slice(h * HEAD, (h + 1) * HEAD)
        x = pre[:, cols]
        res[rows, cols] = (x * cosine + pltpu.roll(x, HEAD // 2, 1) * sine).astype(jnp.bfloat16)


def load_tokens(sc, tok_ref, nodes, pieces, tv, wv, sems):
    deep = pieces[0].shape[0]
    outer, copies = sc[8], []
    for core in range(2):
        for i, node in enumerate(nodes):
            at = pl.multiple_of((2 * sc[node] + (1 - outer if core else outer)) * deep, deep)
            to = (core * len(nodes) + i) * deep
            copies.append((tok_ref.at[:, pl.ds(at, deep)], tv.at[:, to : to + deep]))
            if not core:
                copies.append((pieces[i], wv.at[i * deep : (i + 1) * deep, :]))
    made = [pltpu.make_async_copy(src, dst, sems.at[i]) for i, (src, dst) in enumerate(copies)]
    for c in made:
        c.start()
    return made


def dots(tok, columns, weights):
    total = None
    for at, w in zip(columns, weights):
        part = jnp.dot(tok[:, at : at + w.shape[0]], w[...], preferred_element_type=jnp.float32)
        total = part if total is None else total + part
    return total


def held_keys_kernel(
    sc, count, pos, tok_ref, mine_h, mine_c, y3, a3, given, y3_other, a3_other, tab_ref,
    keys_ref, total_ref, tv, wv, vh, vc, res, sems,
):
    deep, half = y3.shape
    made = load_tokens(sc, tok_ref, (17, 13), (y3, a3), tv, wv, sems)
    made += [pltpu.make_async_copy(mine_h, vh, sems.at[6]), pltpu.make_async_copy(mine_c, vc, sems.at[7])]
    for c in made[6:]:
        c.start()
    for c in made:
        c.wait()
    vc[...] = (vc[...] + given[:, half:]) + dots(tv, (deep, 3 * deep), (wv.at[deep : 2 * deep, :], a3_other))
    last = pltpu.make_async_copy(vc, total_ref, sems.at[8])
    last.start()

    def write(at, cosine, sine):
        pre = dots(tv.at[at, :], (0, 2 * deep), (wv.at[0:deep, :], y3_other))
        rotate_heads(pre + (vh[at, :] + given[at, 0:half]), cosine, sine, res, at)

    rope_blocks(pos, count, tab_ref, vh.shape[0], write)
    save = pltpu.make_async_copy(
        res, keys_ref.at[:, pl.ds(pl.multiple_of(sc[9] * half, half), half)], sems.at[9]
    )
    save.start()
    save.wait()
    last.wait()


def crossed_kernel(
    sc, tok_ref, sib_ref, total_ref, e1, e2, mine_ref, theirs_ref, last_ref, last_sib_ref, tv, wv, vc, sems, out_sems,
):
    deep = e1.shape[0]
    outer, copies = sc[8], []
    columns = lambda node: pl.ds(pl.multiple_of((2 * sc[node] + outer) * deep, deep), deep)
    for i, (node, piece) in enumerate(((15, e1), (16, e2))):
        part = slice(i * deep, (i + 1) * deep)
        copies.append((piece, wv.at[part, :]))
        for k, tok in enumerate((tok_ref, sib_ref)):
            copies.append((tok.at[:, columns(node)], tv.at[k, :, part]))
    copies.append((total_ref, vc.at[0]))
    for i, node in enumerate((17, 14)):
        copies.append((tok_ref.at[:, columns(node)], last_ref.at[i]))
        copies.append((sib_ref.at[:, columns(node)], last_sib_ref.at[i]))
    made = [pltpu.make_async_copy(src, dst, sems.at[i]) for i, (src, dst) in enumerate(copies)]
    for c in made:
        c.start()
    for c in made[:7]:
        c.wait()
    saves = []
    for k, dst in enumerate((mine_ref, theirs_ref)):
        part = jnp.dot(tv[k], wv[...], preferred_element_type=jnp.float32)
        vc[k] = part if k else vc[0] + part
        saves.append(pltpu.make_async_copy(vc.at[k], dst, out_sems.at[k]))
        saves[-1].start()
    for c in made[7:] + saves:
        c.wait()


def last_kernel(total_ref, tok_ref, e3, e0, out_ref):
    total = total_ref[...]
    for i, w in enumerate((e3, e0)):
        total = total + jnp.dot(tok_ref[i], w[...], preferred_element_type=jnp.float32)
    out_ref[...] = total.astype(out_ref.dtype)


def fold_kernel(keep_ref, got_ref, next_ref, *send_refs):
    at = next_ref.shape[0]
    next_ref[...] = keep_ref[0:at] + got_ref[0:at].astype(jnp.float32)
    for ref in send_refs:
        n = ref.shape[0]
        ref[...] = (keep_ref[at : at + n] + got_ref[at : at + n].astype(jnp.float32)).astype(ref.dtype)
        at += n


def sum_kernel(keep_ref, *refs):
    total = keep_ref[...]
    for ref in refs[:-1]:
        total = total + ref[...].astype(jnp.float32)
    refs[-1][...] = total


def crossed_keys_kernel(
    sc, count, pos, total_ref, given, share, share_other, tab_ref, keys_ref, out_ref, down_ref, up_ref, res, sems,
):
    half = total_ref.shape[1]
    outer = sc[8]
    down_rows = down_ref.shape[0] // 2
    up_rows = up_ref.shape[0] // 2
    saves = []

    def save(src, dst):
        c = pltpu.make_async_copy(src, dst, sems.at[len(saves)])
        c.start()
        saves.append(c)

    for core, sums in ((outer, share), (1 - outer, share_other)):
        down_at = pl.multiple_of(core * down_rows, down_rows)
        up_at = pl.multiple_of(core * up_rows, up_rows)
        save(sums.at[0, 0:down_rows, :], down_ref.at[pl.ds(down_at, down_rows), :])
        save(sums.at[0, down_rows:, :], up_ref.at[pl.ds(up_at, up_rows), :])
    columns = pl.ds(pl.multiple_of((1 - sc[9]) * half, half), half)

    def write(at, cosine, sine):
        rotate_heads(total_ref[at, :] + given[at, :].astype(jnp.float32), cosine, sine, res, at)
        save(res.at[at, :], out_ref.at[at, columns])

    rope_blocks(pos, count, tab_ref, res.shape[0], write)
    for c in saves:
        c.wait()


class Routes:
    def __init__(self, mesh):
        self.groups, self.nodes, self.outers = (mesh.shape[a] for a in ALL)
        self.z = self.nodes // 2
        line = list(range(self.z))
        ring = line[:1] + line[1::2] + line[2::2][::-1]
        self.next = {ring[i]: ring[(i + 1) % self.z] for i in range(self.z)}
        self.prev = {v: k for k, v in self.next.items()}

    def pairs(self, f):
        at = lambda g, z, y, o: (g * self.nodes + 2 * z + y) * self.outers + o
        return [
            (at(g, z, y, o), at(*f(g, z, y, o)))
            for g in range(self.groups)
            for z in range(self.z)
            for y in range(2)
            for o in range(self.outers)
        ]

    def table(self):
        rows = []
        for _, n, o, g in [
            (0, n, o, g) for g in range(self.groups) for n in range(self.nodes) for o in range(self.outers)
        ]:
            z, y = divmod(n, 2)
            slot = [n ^ ((r >> 2) & 1 | ((r >> 1) & 1) << 1 | (r & 1) << 2) for r in range(8)]
            from_z = [z]
            for _ in range(self.z - 1):
                from_z.append(self.prev[from_z[-1]])
            rows.append(
                slot + [o, g] + [2 * k + y for k in from_z] + [2 * k + 1 - y for k in from_z]
            )
        return np.array(rows, np.int32)


def call(kernel, name, shapes, in_specs, out_specs, scratch, args, grid=(), prefetch=1, aliases=None, vmem=16):
    specs = [None] * prefetch + in_specs
    return pl.pallas_call(
        kernel,
        out_shape=shapes,
        grid_spec=pltpu.PrefetchScalarGridSpec(
            num_scalar_prefetch=prefetch, grid=grid, in_specs=in_specs, out_specs=out_specs,
            scratch_shapes=scratch,
        ),
        compiler_params=pltpu.CompilerParams(vmem_limit_bytes=vmem * MIB),
        cost_estimate=pl.CostEstimate(flops=1000, bytes_accessed=1024, transcendentals=0),
        input_output_aliases=aliases or {},
        name=name,
    )(*[pltpu.with_memory_space_constraint(x, pltpu.HBM) if spec is HBM else x for x, spec in zip(args, specs)])


def fast_body(
    routes, tokens, frozen_weight, down_adapter, second_adapter_weight, tenant_ids, block_counts, positions, cotangent
):
    bf16, f32 = jnp.bfloat16, jnp.float32
    rows, width = tokens.shape
    deep, kv = frozen_weight.shape
    nodes = routes.nodes
    chunk = 2 * deep
    half = kv // 2
    rank = down_adapter.shape[1]
    plane = lax.axis_index("groups")
    outer = lax.axis_index("outer")
    tab = jnp.asarray(rope_constants())

    send = lambda x, f: lax.ppermute(x, ALL, routes.pairs(f))
    to_core = lambda g, z, y, o: (g, z, y, 1 - o)
    to_x = lambda g, z, y, o: (1 - g, z, y, o)
    to_y = lambda g, z, y, o: (g, z, 1 - y, o)
    to_z = lambda g, z, y, o: (g, routes.next[z], y, o)
    to_z1 = lambda g, z, y, o: (g, z ^ 1, y, o)
    to_z2 = lambda g, z, y, o: (g, z ^ 2, y, o)
    to_z3 = lambda g, z, y, o: (g, z ^ 3, y, o)
    fence = lambda *x: lax.optimization_barrier(x)
    vm = pl.BlockSpec(memory_space=pltpu.VMEM)
    dma = pltpu.SemaphoreType.DMA
    shape = jax.ShapeDtypeStruct

    def fold(keep, got, stay, *go):
        slots = lambda n, dtype: pltpu.VMEM((n, *keep.shape[1:]), dtype)
        return call(
            fold_kernel, "fold", [slots(stay, f32), *[slots(n, bf16) for n in go]],
            [vm, vm], [vm] * (1 + len(go)), [], (keep, got), prefetch=0,
        )

    def product(held, crossed, given=(), adapters=(), joined=False):
        kh, kc = len(held) * deep, max(len(crossed), 1) * deep
        outs = [pltpu.VMEM((rows, half), f32)] * (2 if crossed else 1)
        outs += [pltpu.VMEM((rows, kv), f32)] if joined else outs
        return call(
            functools.partial(
                product_kernel, [i for _, i in held], [i for _, i in crossed], not given, joined
            ),
            "products", outs,
            [HBM] * 2 + [HBM if w is frozen_weight else ANY for w, _ in held + crossed] + [ANY] * len(given)
            + [vm] * len(adapters), [ANY] * len(outs),
            [
                pltpu.VMEM((2, rows, kh), bf16), pltpu.VMEM((2, rows, kc), bf16),
                pltpu.VMEM((kh, half), bf16), pltpu.VMEM((kc, half), bf16),
                pltpu.VMEM((2, rows, half), f32), pltpu.VMEM((2, rows, half), f32),
                dma((3 * len(held) + 3 * len(crossed) + 4,)), dma((5,)),
            ],
            (sc, tokens, sib_tokens, *[w for w, _ in held], *[w for w, _ in crossed], *given, *adapters),
        )

    z0 = lax.dynamic_slice(frozen_weight, (0, plane * half), (deep, half))
    z0, own_tokens, table = fence(z0, tokens, jnp.asarray(routes.table()))
    sc = lax.dynamic_slice(table, (lax.axis_index(ALL), 0), (1, table.shape[1]))[0]
    z1 = send(z0, to_z)
    y0 = send(z0, to_y)
    sib_tokens = send(own_tokens, to_core)
    slot_rows = chunk // 2 + kv // nodes // 2
    low, own, sib = call(
        gradient_kernel, "adapter_gradients",
        [
            pltpu.VMEM((rows, rank), bf16), pltpu.VMEM((nodes, slot_rows, rank), f32),
            pltpu.VMEM((nodes, slot_rows, rank), bf16),
        ],
        [HBM] * 5, [vm] * 3,
        [
            pltpu.VMEM((nodes, rows, chunk), bf16), pltpu.VMEM((nodes, chunk, rank), bf16),
            pltpu.VMEM((kv, rank), bf16), pltpu.VMEM((nodes, rows, HEAD), bf16), pltpu.VMEM(tab.shape, f32),
            pltpu.VMEM((rows, HEAD), f32), pltpu.VMEM((rows, HEAD), f32), pltpu.VMEM((nodes, rows, HEAD), bf16),
            pltpu.VMEM((rows, rank), f32), pltpu.VMEM((rows, rank), f32), pltpu.VMEM((HEAD, rank), f32),
            dma((4, nodes)),
        ],
        (sc, tenant_ids, block_counts, positions, tokens, down_adapter, second_adapter_weight, cotangent, tab),
        prefetch=4, vmem=52,
    )
    z1, y0, low, own, sib, sib_tokens = fence(z1, y0, low, own, sib, sib_tokens)

    def own_crossed(core, *given):
        return call(
            functools.partial(own_crossed_kernel, core, len(given)), "own_crossed",
            [pltpu.VMEM((rows, half), f32)] * 2 + [pltpu.VMEM((deep, half), bf16)],
            [HBM] * 3 + [vm] * (2 + len(given)), [vm] * 3, [pltpu.VMEM((2, rows, deep), bf16), dma((3,))],
            (sc, tokens, sib_tokens, frozen_weight, low, second_adapter_weight, *given),
            aliases={6 + i: i for i in range(len(given))},
        )

    other = send(sib, to_core)
    started = own_crossed(0)
    z1, *started = fence(z1, *started)
    z2 = send(z1, to_z)
    y1 = send(z1, to_y)
    a1 = send(z1, to_x)
    crossed_sum, crossed_sib, c0 = own_crossed(1, *started)
    held_sum, held_sib = product(
        ((frozen_weight, 10), (y0, 14), (z1, 11)), (), adapters=(low, second_adapter_weight)
    )
    totals = held_sum, crossed_sum, held_sib, crossed_sib
    z2, other, *totals = fence(z2, other, *totals)

    z3 = send(z2, to_z)
    y2 = send(z2, to_y)
    a2 = send(z2, to_x)
    keep, out = fold(own, other, 4, 4)
    totals = product(((y1, 15), (z2, 12)), ((a1, 11),), given=totals)
    z3, y2, a2, keep, out, *totals = fence(z3, y2, a2, keep, out, *totals)

    y3 = send(y2, to_z)
    a3 = send(z3, to_x)
    got = send(out, to_y)
    mine_h, mine_c, theirs = product(((y2, 16), (z3, 13)), ((a2, 12),), given=totals, joined=True)
    y3, a3, got, mine_h, mine_c, theirs = fence(y3, a3, got, mine_h, mine_c, theirs)

    given, y3_other, a3_other = send(theirs, to_core), send(y3, to_core), send(a3, to_core)
    e1 = send(y1, to_x)
    e2 = send(a2, to_y)
    keep, *out = fold(keep, got, 1, 1, 1, 1)
    got = [send(x, f) for x, f in zip(out, (to_z2, to_z1, to_z3))]
    own_space = [
        pltpu.VMEM((rows, 2 * chunk), bf16), pltpu.VMEM((chunk, half), bf16), pltpu.VMEM((rows, half), f32),
    ]
    keys, total = call(
        held_keys_kernel, "held_keys", [shape((rows, kv), bf16), pltpu.VMEM((rows, half), f32)],
        [HBM] + [ANY] * 4 + [vm] * 4, [ANY, ANY],
        own_space + [pltpu.VMEM((rows, half), f32), pltpu.VMEM((rows, half), bf16), dma((10,))],
        (sc, block_counts, positions, tokens, mine_h, mine_c, y3, a3, given, y3_other, a3_other, tab),
        prefetch=3,
    )
    y3, c0, total = fence(y3, c0, total)
    e3 = send(y3, to_x)
    e0 = send(c0, to_y)
    e1, e2, total = fence(e1, e2, total)
    *sums, last, last_sib = call(
        crossed_kernel, "crossed_products",
        [pltpu.VMEM((rows, half), f32)] * 2 + [pltpu.VMEM((2, rows, deep), bf16)] * 2,
        [HBM] * 2 + [ANY] * 3, [ANY] * 4,
        [
            pltpu.VMEM((2, rows, chunk), bf16), pltpu.VMEM((chunk, half), bf16),
            pltpu.VMEM((2, rows, half), f32), dma((11,)), dma((2,)),
        ],
        (sc, tokens, sib_tokens, total, e1, e2),
    )
    e3, e0, mine, theirs, last, last_sib, *got = fence(e3, e0, *sums, last, last_sib, *got)

    share = call(
        sum_kernel, "share", pltpu.VMEM(keep.shape, f32), [vm] * 4, vm, [], (keep, *got), prefetch=0,
    )
    finish = lambda total, toks, dtype: call(
        last_kernel, "last_product", pltpu.VMEM((rows, half), dtype), [vm] * 4, vm, [], (total, toks, e3, e0), prefetch=0,
    )
    given = send(finish(theirs, last_sib, bf16), to_core)
    keys, down, up = call(
        crossed_keys_kernel, "crossed_keys",
        [shape((rows, kv), bf16), shape((chunk, rank), f32), shape((kv // nodes, rank), f32)],
        [vm] * 5 + [ANY], [ANY] * 3,
        [pltpu.VMEM((rows, half), bf16), dma((4 + rows // BLK,))],
        (
            sc, block_counts, positions, finish(mine, last, f32), given, share, send(share, to_core), tab, keys,
        ),
        prefetch=3, aliases={8: 0},
    )
    return keys, down, up


def rope_tables(positions):
    half_head = HEAD // 2
    frequency = ROPE_BASE ** (-2.0 * jnp.arange(half_head, dtype=jnp.float32) / HEAD)
    angle = positions.astype(jnp.float32)[:, None] * frequency[None, :]
    return (jnp.cos(angle), jnp.sin(angle))


def rotate(field, cosine, sine, orient):
    rows = field.shape[0]
    shaped = field.reshape(rows, -1, 2, HEAD // 2)
    first = shaped[:, :, 0]
    second = shaped[:, :, 1]
    cos_b = cosine[:, None, :]
    sin_b = orient * sine[:, None, :]
    out_first = first * cos_b - second * sin_b
    out_second = second * cos_b + first * sin_b
    return jnp.stack((out_first, out_second), axis=2).reshape(rows, -1)


def plain_body(
    tokens, frozen_weight, down_adapter, second_adapter_weight, tenant_ids, block_counts, positions, cotangent
):
    token_rows = tokens.shape[0]
    block_total = tenant_ids.shape[0]
    block_rows = token_rows // block_total
    width_cols = down_adapter.shape[1]
    live_blocks = (jnp.arange(block_total, dtype=jnp.int32) < block_counts[0]).astype(jnp.float32)
    live_rows = jnp.repeat(live_blocks, block_rows)[:, None]
    column_tenant = jnp.arange(width_cols, dtype=jnp.int32) // R
    select_blocks = (tenant_ids[:, None] == column_tenant[None, :]).astype(
        jnp.float32
    ) * live_blocks[:, None]
    select = jnp.repeat(select_blocks, block_rows, axis=0)
    lowrank_hidden = (
        jnp.dot(tokens, down_adapter, preferred_element_type=jnp.float32) * select
    ).astype(jnp.bfloat16)
    frozen_output = jnp.dot(
        tokens,
        lax.all_gather(frozen_weight, ("node", "outer"), axis=0, tiled=True),
        preferred_element_type=jnp.float32,
    )
    adapter_output = lax.dot_general(
        lowrank_hidden,
        second_adapter_weight,
        (((1,), (1,)), ((), ())),
        preferred_element_type=jnp.float32,
    )
    unrotated_keys = frozen_output + ADAPTER_SCALE * adapter_output
    cosine, sine = rope_tables(positions)
    keys = (live_rows * rotate(unrotated_keys, cosine, sine, 1.0)).astype(jnp.bfloat16)
    output_gradient = (
        live_rows * rotate(cotangent.astype(jnp.float32), cosine, sine, -1.0)
    ).astype(jnp.bfloat16)
    backward_gradient = (
        jnp.dot(output_gradient, second_adapter_weight, preferred_element_type=jnp.float32) * select
    ).astype(jnp.bfloat16)
    down_product = ADAPTER_SCALE * lax.dot_general(
        tokens, backward_gradient, (((0,), (0,)), ((), ())), preferred_element_type=jnp.float32
    )
    up_product = ADAPTER_SCALE * lax.dot_general(
        output_gradient,
        lowrank_hidden,
        (((0,), (0,)), ((), ())),
        preferred_element_type=jnp.float32,
    )
    shares = (
        lax.psum_scatter(down_product, "node", scatter_dimension=0, tiled=True),
        lax.psum_scatter(up_product, "node", scatter_dimension=0, tiled=True),
    )
    down_adapter_gradient, up_adapter_gradient = lax.psum((shares[0], shares[1]), "outer")
    return (keys, down_adapter_gradient, up_adapter_gradient)


def solution(mesh):
    placed = (
        P(("groups", "node", "outer"), None),
        P(("node", "outer"), None),
        P(),
        P(),
        P(("groups", "node", "outer")),
        P(("groups", "node", "outer")),
        P(("groups", "node", "outer")),
        P(("groups", "node", "outer"), None),
    )
    routed = tuple(mesh.shape[a] for a in ALL) == (2, 8, 2)
    return jax.shard_map(
        functools.partial(fast_body, Routes(mesh)) if routed else plain_body,
        mesh=mesh,
        in_specs=placed,
        out_specs=(
            P(("groups", "node", "outer"), None),
            P(("groups", "node"), None),
            P(("groups", "node"), None),
        ),
        check_vma=False,
    )
```
